32 devices in a mesh: shot: 8 (over z, x), sub: 4 (over y, core).
Axes of the slice: x: 2, y: 2, z: 4, core: 2. Of those that a mesh axis runs over, the one named last changes fastest.
Arguments:
- stiffness: float32 [64, 32, 384], P('sub'), may hold values from 0.04 to 0.15
- buoyancy_first: float32 [64, 32, 384], P('sub'), may hold values from 0.6 to 1.3
- buoyancy_second: float32 [64, 32, 384], P('sub'), may hold values from 0.6 to 1.3
- buoyancy_third: float32 [64, 32, 384], P('sub'), may hold values from 0.6 to 1.3
- adjoint_before: float32 [8, 64, 32, 384], P('shot', 'sub'), may hold values from -6 to 6
- adjoint_current: float32 [8, 64, 32, 384], P('shot', 'sub'), may hold values from -6 to 6
- forward_field: bfloat16 [8, 8, 64, 32, 384], P('shot', None, 'sub'), may hold values from -6 to 6
- traces: float32 [16384, 256], P(('shot', 'sub')), may hold values from -6 to 6
- receiver_target: int32 [16384, 1], P(('shot', 'sub')), may hold values from 0 to 31; in each aligned block of 512 rows (0 to 511, 512 to 1023, ...) at most 24 rows name the same one
- receiver_cell: int32 [16384], P(('shot', 'sub')), may hold values from 0 to 196607
- source_cell: int32 [8, 3], P('shot'), may hold values from 0 to 31
Outputs:
- gradient: float32 [64, 12288], P('sub', 'shot')
- adjoint_earlier: float32 [8, 64, 32, 384], P('shot', 'sub')
- adjoint_latest: float32 [8, 64, 32, 384], P('shot', 'sub')
The draws below stay inside these ranges and needn't reach their ends.
Inputs may be any that keep to these rules, and one draw needn't show every extreme that they name: `receiver_target`: at most 24 of the receivers stored on one device share a value, and 24 is reached. `receiver_cell`: flattened with the first dimension slowest.
All inputs are finite; a program needn't handle non-finite values.
Results may differ from the reference program's by a relative error of at most 0.0003.
Values sent between devices are 32-bit elements; how exact they have to be, the bound alone decides.
A program may use at most 128 MiB of HBM per device.

```python
import math
import jax
import jax.numpy as jnp
import numpy as np
from jax import lax

CX = 16
NY = 32
NZ = 384
STEPS = 8
SAMPLES = 256
R_DEV = 512
MUTE = 6
NX = 64
CELLS = 196608
GROUPS = 8
R_ALL = 16384
CAP = 24
N_SHOT = 8
N_SUB = 4
DEVICES = 32


def set_ends(entries, key, least, high):
    longest = entries.shape.index(max(entries.shape))
    spots = []
    for shift in (0, 1):
        where = [jax.random.randint(jax.random.fold_in(key, axis), (), 0, length) for axis, length in enumerate(entries.shape)]
        where[longest] = (where[longest] + shift) % entries.shape[longest]
        spots.append(tuple(where))
    return entries.at[spots[0]].set(least).at[spots[1]].set(high)


def shard_levels(rng, shape, shards, least, top_value):
    def one(dim, blocks):
        draws = jax.random.uniform(jax.random.fold_in(jax.random.fold_in(rng, 6), dim), (blocks,), jnp.float32, least / len(shards), top_value / len(shards))
        return jnp.repeat(jnp.exp(draws), shape[dim] // blocks).reshape((-1,) + (1,) * (len(shape) - dim - 1))

    factor_of = one(*shards[0])
    for cut in shards[1:]:
        factor_of = factor_of * one(*cut)
    return factor_of


def assign_block(stream_key, own, number, rows, number_of, top, bound, lean):
    sequence = jax.random.permutation(stream_key, number_of)
    crowded, ordinary = shares(number_of, rows * top, bound, lean, True), shares(number_of, rows * top, bound, lean, False)
    places = jnp.arange(number_of)

    def named(tallies, rotation):
        used = int((tallies > 0).sum())
        fixed = max(1, used // 4)
        moved = fixed + (places - fixed + rotation * (used - fixed)) % max(1, number_of - fixed)
        return jnp.zeros((number_of,), jnp.int32).at[sequence[jnp.where(places < fixed, places, moved)]].set(jnp.asarray(tallies, jnp.int32))

    tallies = jnp.where(number % 4 == 0, named(crowded, number // 4), named(ordinary, number - number // 4 - 1))
    mixed = jax.random.permutation(jax.random.fold_in(own, 3), number_of)
    source_of, sink = mixed[0:number_of // 2 * 2:2], mixed[1:number_of // 2 * 2:2]
    margin = jnp.minimum(tallies[source_of] - 1, bound - tallies[sink]) // 2
    margin = jnp.where((source_of == sequence[0]) | (sink == sequence[0]) | (tallies[sink] == 0), 0, jnp.maximum(margin, 0))
    moved = jax.random.randint(jax.random.fold_in(own, 4), (number_of // 2,), 0, 1 << 20) % (margin + 1)
    tallies = tallies.at[source_of].add(-moved).at[sink].add(moved)
    labels = jnp.searchsorted(jnp.cumsum(tallies), jnp.arange(rows * top), side="right").astype(jnp.int32)
    grid = labels.reshape(top, rows).T
    grid = grid[jax.random.permutation(jax.random.fold_in(own, 1), rows)]
    rotation = jax.random.randint(jax.random.fold_in(own, 2), (rows, 1), 0, top)
    return jnp.take_along_axis(grid, (jnp.arange(top)[None, :] + rotation) % top, axis=1)


def shares(count, total, limit, slope, full):
    portions = [(1 << 20) // math.isqrt(standing ** slope) + 1 for standing in range(1, count + 1)]
    largest = limit if full else min(limit, max(-(-total // count), total * portions[0] // sum(portions)))
    least = 1 if total - largest >= count - 1 else 0
    given, surplus = [largest] + [least] * (count - 1), total - largest - least * (count - 1)
    while surplus > 0:
        movable = [i for i in range(1, count) if given[i] < largest] or [i for i in range(1, count) if given[i] < limit]
        pool, remaining = sum([portions[i] for i in movable]), surplus
        for i in movable:
            more = min(limit - given[i], max(1, remaining * portions[i] // pool), surplus)
            given[i] = given[i] + more
            surplus = surplus - more
    return np.array(given)


def normal_values(own_key, shape, spread, reach, pieces=(), held_as=jnp.bfloat16):
    gain = shard_levels(own_key, shape, pieces, -0.22, 0.18) if pieces else 1.0
    drawn = jax.random.normal(own_key, shape, jnp.float32) * spread * gain
    return jnp.minimum(jnp.maximum(drawn, -reach), reach).astype(held_as)


def setup_inputs(seed: int = 0) -> dict:
    keys = jax.random.split(jax.random.key(seed), 12)
    stiffness = jnp.clip(jnp.exp(math.log(0.15) - 1.3217559 * jax.random.uniform(keys[0], (NX, NY, NZ), jnp.float32) ** shard_levels(keys[0], (NX, NY, NZ), ((0, 4),), -0.2, 0.2)), 0.04, 0.15)
    buoyancy_first = jnp.clip(jnp.exp(math.log(1.3) - 0.7731898 * jax.random.uniform(keys[1], (NX, NY, NZ), jnp.float32) ** shard_levels(keys[1], (NX, NY, NZ), ((0, 4),), -0.2, 0.2)), 0.6, 1.3)
    buoyancy_second = jnp.clip(jnp.exp(math.log(1.3) - 0.7731898 * jax.random.uniform(keys[2], (NX, NY, NZ), jnp.float32) ** shard_levels(keys[2], (NX, NY, NZ), ((0, 4),), -0.2, 0.2)), 0.6, 1.3)
    buoyancy_third = jnp.clip(jnp.exp(math.log(1.3) - 0.7731898 * jax.random.uniform(keys[3], (NX, NY, NZ), jnp.float32) ** shard_levels(keys[3], (NX, NY, NZ), ((0, 4),), -0.2, 0.2)), 0.6, 1.3)
    adjoint_before = normal_values(keys[4], (GROUPS, NX, NY, NZ), 1.0, 6.0, ((0, 8), (1, 4)), jnp.float32)
    adjoint_current = normal_values(keys[5], (GROUPS, NX, NY, NZ), 1.0, 6.0, ((0, 8), (1, 4)), jnp.float32)
    forward_field = normal_values(keys[6], (GROUPS, STEPS, NX, NY, NZ), 1.0, 6.0, ((0, 8), (2, 4)))
    traces = normal_values(keys[7], (R_ALL, SAMPLES), 1.0, 6.0, ((0, 32),), jnp.float32)
    receiver_target_keys = jax.random.split(jax.random.fold_in(keys[8], 1), R_ALL // R_DEV)
    receiver_target_turns = jax.random.permutation(jax.random.fold_in(keys[8], 3), R_ALL // R_DEV)
    receiver_target = jax.vmap(lambda own, number: assign_block(jax.random.fold_in(keys[8], 2), own, number, R_DEV, DEVICES, 1, CAP, 2))(receiver_target_keys, receiver_target_turns).reshape((R_ALL, 1))
    receiver_cell = set_ends(jax.random.randint(keys[9], (R_ALL,), 0, CELLS), jax.random.fold_in(keys[9], 1), 0, CELLS - 1).astype(jnp.int32)
    source_cell = set_ends(jax.random.randint(keys[10], (GROUPS, 3), 0, min(NX, min(NY, NZ))), jax.random.fold_in(keys[10], 1), 0, (min(NX, min(NY, NZ))) - 1).astype(jnp.int32)
    return dict(stiffness=stiffness, buoyancy_first=buoyancy_first, buoyancy_second=buoyancy_second, buoyancy_third=buoyancy_third, adjoint_before=adjoint_before, adjoint_current=adjoint_current, forward_field=forward_field, traces=traces, receiver_target=receiver_target, receiver_cell=receiver_cell, source_cell=source_cell)


COEFFS = (1225.0 / 1024.0, -245.0 / 3072.0, 49.0 / 5120.0, -5.0 / 7168.0)
DAMP = 0.1


def take_slice(extended, dimension, offset, length):
    return lax.slice_in_dim(extended, offset, offset + length, axis=dimension)


def forward_difference(extended, dimension, offset, length):
    summed = COEFFS[0] * (take_slice(extended, dimension, offset + 1, length) - take_slice(extended, dimension, offset, length))
    for order in range(2, 5):
        summed = summed + COEFFS[order - 1] * (take_slice(extended, dimension, offset + order, length) - take_slice(extended, dimension, offset + 1 - order, length))
    return summed


def backward_difference(extended, dimension, offset, length):
    summed = COEFFS[0] * (take_slice(extended, dimension, offset, length) - take_slice(extended, dimension, offset - 1, length))
    for order in range(2, 5):
        summed = summed + COEFFS[order - 1] * (take_slice(extended, dimension, offset + order - 1, length) - take_slice(extended, dimension, offset - order, length))
    return summed


def pad_along(wave_field, dimension, amount):
    widths = [(0, 0)] * wave_field.ndim
    widths[dimension] = (amount, amount)
    return jnp.pad(wave_field, widths)


def local_divergence(wave_field, buoyancy, dimension):
    length = wave_field.shape[dimension]
    flux_field = buoyancy * forward_difference(pad_along(wave_field, dimension, 4), dimension, 4, length)
    return backward_difference(pad_along(flux_field, dimension, 4), dimension, 4, length)


def trace_kernel(sample_count, step_count):
    sample_pos = jnp.arange(sample_count, dtype=jnp.float32)[:, None]
    centers = (jnp.arange(step_count, dtype=jnp.float32)[None, :] + 0.5) * (sample_count / step_count)
    return 0.25 * jnp.exp(-jnp.abs(sample_pos - centers) / (sample_count / 8.0))


def reference(stiffness, buoyancy_first, buoyancy_second, buoyancy_third, adjoint_before, adjoint_current, forward_field, traces, receiver_target, receiver_cell, source_cell):
    kernel = trace_kernel(SAMPLES, STEPS)
    values = jnp.dot(traces, kernel, precision=lax.Precision.HIGHEST, preferred_element_type=jnp.float32)
    target = receiver_target[:, 0]
    group_of = target // N_SUB
    flat_cell = ((target % N_SUB) * (CX * NY * NZ) + receiver_cell).astype(jnp.int32)
    total_cells = NX * NY * NZ
    coord_first = jnp.arange(NX, dtype=jnp.float32)[:, None, None]
    coord_second = jnp.arange(NY, dtype=jnp.float32)[None, :, None]
    coord_third = jnp.arange(NZ, dtype=jnp.float32)[None, None, :]

    def one_group(carry, packed):
        summed_image, summed_light = carry
        group_id, earlier, current, forward_now, source_at = packed
        belongs = group_of == group_id
        chosen = jnp.where(belongs[:, None], values, jnp.float32(0.0))
        injection = jnp.zeros((STEPS, total_cells), jnp.float32).at[:, flat_cell].add(chosen.T)
        image_sum = jnp.zeros((NX, NY, NZ), jnp.float32)
        illumination = jnp.zeros((NX, NY, NZ), jnp.float32)
        for moment in range(STEPS):
            divergence = local_divergence(current, buoyancy_first, 0)
            divergence = divergence + local_divergence(current, buoyancy_second, 1)
            divergence = divergence + local_divergence(current, buoyancy_third, 2)
            change = stiffness * divergence + injection[moment].reshape(NX, NY, NZ)
            following = 2.0 * current - earlier + change
            frame = forward_now[moment].astype(jnp.float32)
            image_sum = image_sum + frame * change
            illumination = illumination + frame * frame
            earlier, current = current, following
        source_pos = source_at.astype(jnp.float32)
        distance = (coord_first - source_pos[0]) ** 2 + (coord_second - source_pos[1]) ** 2 + (coord_third - source_pos[2]) ** 2
        mute_weight = 1.0 - jnp.exp(-distance / (2.0 * MUTE * MUTE))
        return (summed_image + mute_weight * image_sum, summed_light + illumination), (earlier, current)

    start = (jnp.zeros((NX, NY, NZ), jnp.float32), jnp.zeros((NX, NY, NZ), jnp.float32))
    packed = (jnp.arange(GROUPS, dtype=jnp.int32), adjoint_before, adjoint_current, forward_field, source_cell)
    (summed_image, summed_light), (earliers, latests) = lax.scan(one_group, start, packed)
    gradient = summed_image / (summed_light / (STEPS * N_SHOT) + DAMP)
    return gradient.reshape(NX, NY * NZ), earliers, latests
```

```python
import functools

import jax
import jax.numpy as jnp
from jax import lax
from jax.experimental import pallas as pl
from jax.experimental.pallas import tpu as pltpu
from jax.sharding import PartitionSpec as P

MUTE = 6
COEFFS = (1225.0 / 1024.0, -245.0 / 3072.0, 49.0 / 5120.0, -5.0 / 7168.0)
RATIOS = tuple(c / COEFFS[0] for c in COEFFS)
SCALE = COEFFS[0] * COEFFS[0]
DAMP = 0.1
LANES = 128
HALO = 7
PAD = 8
MESH = pl.DeviceIdType.MESH


def trace_kernel(sample_count, step_count):
    sample_pos = jnp.arange(sample_count, dtype=jnp.float32)[:, None]
    centers = (jnp.arange(step_count, dtype=jnp.float32)[None, :] + 0.5) * (
        sample_count / step_count
    )
    return 0.25 * jnp.exp(-jnp.abs(sample_pos - centers) / (sample_count / 8.0))


def weighted(pairs):
    total = pairs[0][0] - pairs[0][1]
    for ratio, (ahead, behind) in zip(RATIOS[1:], pairs[1:]):
        total = total + ratio * (ahead - behind)
    return total


def shifted(chunks, amount, lane):
    if amount == 0:
        return chunks
    rolled = [pltpu.roll(chunk, (-amount) % LANES, 1) for chunk in chunks]
    zero = jnp.zeros_like(chunks[0])
    out = []
    for c in range(len(chunks)):
        if amount > 0:
            other = rolled[c + 1] if c + 1 < len(chunks) else zero
            out.append(jnp.where(lane < LANES - amount, rolled[c], other))
        else:
            other = rolled[c - 1] if c > 0 else zero
            out.append(jnp.where(lane >= -amount, rolled[c], other))
    return out


def scatter_body(chunk_count, plane_rows, place_ref, value_ref, dense_ref):
    dense_ref[...] = jnp.zeros_like(dense_ref)
    lane = lax.broadcasted_iota(jnp.int32, (8, LANES), 1)

    def block(group, carry):
        tile = value_ref[group]

        def one(slot, inner):
            cell = place_ref[group * LANES + slot]
            spot = cell // LANES
            at = cell - spot * LANES
            row = (spot % chunk_count) * plane_rows + spot // chunk_count
            moved = pltpu.roll(tile, (at - slot + LANES) % LANES, 1)
            dense_ref[row] = dense_ref[row] + jnp.where(lane == at, moved, 0.0)
            return inner

        return lax.fori_loop(0, LANES, one, carry, unroll=8)

    lax.fori_loop(0, value_ref.shape[0], block, 0)


def wave_body(
    dims,
    stiff_hbm, first_hbm, second_hbm, third_hbm, before_hbm, current_hbm, forward_hbm,
    inject_hbm, source_ref,
    image_out, light_out, earlier_out, latest_out,
    field, stiff, first, second, third, partial, image, light, forward, inject, flux,
    load_sem, store_sem, edge_send, edge_recv, face_send, face_recv,
):
    steps, depth, rows, chunk_count = dims
    sub = lax.axis_index("sub")
    ends = lax.axis_size("sub") - 1
    has_left = sub > 0
    has_right = sub < ends
    zero_tile = jnp.zeros((8, LANES), jnp.float32)

    for c in range(chunk_count):
        def clear(plane, carry, c=c):
            for b in range(2):
                field[b, c, plane, 0:PAD, :] = zero_tile
                field[b, c, plane, PAD + rows:2 * PAD + rows, :] = zero_tile
            return carry
        lax.fori_loop(HALO, HALO + depth, clear, 0)
        for plane in list(range(HALO)) + list(range(HALO + depth, 2 * HALO + depth)):
            for b in range(2):
                field[b, c, plane] = jnp.zeros((2 * PAD + rows, LANES), jnp.float32)
        for face in list(range(4)) + list(range(4 + depth, 7 + depth)):
            first[c, face] = jnp.zeros((rows, LANES), jnp.float32)
        flux[c] = jnp.zeros((2 * PAD + rows, LANES), jnp.float32)

    barrier = pltpu.get_barrier_semaphore()

    @pl.when(has_left)
    def _():
        pl.semaphore_signal(barrier, inc=1, device_id={"sub": sub - 1}, device_id_type=MESH)

    @pl.when(has_right)
    def _():
        pl.semaphore_signal(barrier, inc=1, device_id={"sub": sub + 1}, device_id_type=MESH)

    def lanes(c):
        return pl.ds(c * LANES, LANES)

    inner = pl.ds(PAD, rows)
    loads = []

    def load(src, dst):
        copy = pltpu.make_async_copy(src, dst, load_sem.at[len(loads)])
        copy.start()
        loads.append(copy)

    for c in range(chunk_count):
        load(current_hbm.at[:, :, lanes(c)], field.at[0, c, pl.ds(HALO, depth), inner, :])
        load(third_hbm.at[:, :, lanes(c)], third.at[c])
        load(second_hbm.at[:, :, lanes(c)], second.at[c])
    early = len(loads)
    load(forward_hbm, forward)
    for c in range(chunk_count):
        load(first_hbm.at[:, :, lanes(c)], first.at[c, pl.ds(4, depth)])
        load(stiff_hbm.at[:, :, lanes(c)], stiff.at[c])
        load(before_hbm.at[:, :, lanes(c)], field.at[1, c, pl.ds(HALO, depth), inner, :])
    load(inject_hbm, inject)

    pl.semaphore_wait(barrier, jnp.where(has_left, 1, 0) + jnp.where(has_right, 1, 0))

    def face_copy(side, c):
        if side == 0:
            src = first_hbm.at[pl.ds(0, 3), :, lanes(c)]
            dst = first.at[c, pl.ds(4 + depth, 3)]
            to = sub - 1
        else:
            src = first_hbm.at[pl.ds(depth - 4, 4), :, lanes(c)]
            dst = first.at[c, pl.ds(0, 4)]
            to = sub + 1
        return pltpu.make_async_remote_copy(
            src, dst, face_send.at[side, c], face_recv.at[side, c],
            device_id={"sub": to}, device_id_type=MESH)

    def edge_copy(side, c, b, from_hbm=False):
        start = 0 if side == 0 else depth - HALO
        if from_hbm:
            src = current_hbm.at[pl.ds(start, HALO), :, lanes(c)]
        else:
            src = field.at[b, c, pl.ds(HALO + start, HALO), inner, :]
        dst = field.at[b, c, pl.ds(HALO + depth if side == 0 else 0, HALO), inner, :]
        return pltpu.make_async_remote_copy(
            src, dst, edge_send.at[side, c, b], edge_recv.at[side, c, b],
            device_id={"sub": sub - 1 if side == 0 else sub + 1}, device_id_type=MESH)

    sends_on = (has_left, has_right)
    gets_on = (has_right, has_left)
    for c in range(chunk_count):
        for side in range(2):
            @pl.when(sends_on[side])
            def _(side=side, c=c):
                edge_copy(side, c, 0, True).start()
                face_copy(side, c).start()

    lane = lax.broadcasted_iota(jnp.int32, (8, LANES), 1)
    for copy in loads[:early]:
        copy.wait()

    def inner_part(b, x, carry):
        for y in range(0, rows, 8):
            at = pl.ds(y, 8)
            p = [field[b, c, HALO + x, pl.ds(PAD + y, 8), :] for c in range(chunk_count)]
            pairs = [(shifted(p, k, lane), shifted(p, 1 - k, lane)) for k in range(1, 5)]
            q = [
                third[c, x, at, :] * weighted([(a[c], z[c]) for a, z in pairs])
                for c in range(chunk_count)
            ]
            pairs = [(shifted(q, k - 1, lane), shifted(q, -k, lane)) for k in range(1, 5)]
            for c in range(chunk_count):
                partial[c, x, at, :] = weighted([(a[c], z[c]) for a, z in pairs])
        for c in range(chunk_count):
            for y in range(0, rows, 8):
                def near(s, c=c, y=y):
                    return field[b, c, HALO + x, pl.ds(PAD + y + s, 8), :]
                flux[c, pl.ds(PAD + y, 8), :] = second[c, x, pl.ds(y, 8), :] * weighted(
                    [(near(k), near(1 - k)) for k in range(1, 5)])
        for c in range(chunk_count):
            for y in range(0, rows, 8):
                def near(s, c=c, y=y):
                    return flux[c, pl.ds(PAD + y + s, 8), :]
                at = pl.ds(y, 8)
                partial[c, x, at, :] = partial[c, x, at, :] + weighted(
                    [(near(k - 1), near(-k)) for k in range(1, 5)])
        return carry

    def inner_all(b):
        lax.fori_loop(0, depth, functools.partial(inner_part, b), 0)

    inner_all(0)
    for copy in loads[early:]:
        copy.wait()

    def prepare(x, carry):
        for c in range(chunk_count):
            stiff[c, x] = stiff[c, x] * SCALE
            total = jnp.zeros((rows, LANES), jnp.float32)
            for t in range(steps):
                frame = forward[t, x, :, c * LANES:(c + 1) * LANES].astype(jnp.float32)
                total = total + frame * frame
            light[c, x] = total
            image[c, x] = jnp.zeros((rows, LANES), jnp.float32)
        return carry

    lax.fori_loop(0, depth, prepare, 0)

    for c in range(chunk_count):
        for side in range(2):
            @pl.when(gets_on[side])
            def _(side=side, c=c):
                face_copy(side, c).wait_recv()

            @pl.when(sends_on[side])
            def _(side=side, c=c):
                face_copy(side, c).wait_send()

    def outer_part(c, t, b, half, carry):
        y = pl.multiple_of(half * 16, 16)
        at = pl.ds(y, 16)
        wide = pl.ds(pl.multiple_of(PAD + y, 8), 16)
        p = [field[b, c, i, wide, :] for i in range(8)]
        q = []
        for f in range(-4, depth + 3):
            q.append(first[c, f + 4, at, :] * weighted([(p[3 + k], p[4 - k]) for k in range(1, 5)]))
            x = f - 3
            if x >= 0:
                div = weighted([(q[3 + k], q[4 - k]) for k in range(1, 5)]) + partial[c, x, at, :]
                change = stiff[c, x, at, :] * div + inject[c, x, pl.ds(t + 8 * y, 16, stride=8), :]
                now = p[0]
                past = field[1 - b, c, HALO + x, wide, :]
                field[1 - b, c, HALO + x, wide, :] = (now + now) - past + change
                frame = forward[t, x, at, c * LANES:(c + 1) * LANES].astype(jnp.float32)
                image[c, x, at, :] = image[c, x, at, :] + frame * change
                q = q[1:]
            if f + 1 < depth + 3:
                p = p[1:] + [field[b, c, f + 5 + HALO, wide, :]]
        return carry

    def one_step(t, carry):
        b = lax.rem(t, 2)

        @pl.when(t > 0)
        def _():
            inner_all(b)

        for c in range(chunk_count):
            for side in range(2):
                @pl.when(gets_on[side])
                def _(side=side, c=c):
                    edge_copy(side, c, b).wait_recv()

                @pl.when(sends_on[side])
                def _(side=side, c=c):
                    edge_copy(side, c, b).wait_send()

            lax.fori_loop(0, rows // 16, functools.partial(outer_part, c, t, b), 0)
            for side in range(2):
                @pl.when(jnp.logical_and(sends_on[side], t < steps - 1))
                def _(side=side, c=c):
                    edge_copy(side, c, 1 - b).start()
        return carry

    lax.fori_loop(0, steps, one_step, 0)

    stores = []

    def store(src, dst):
        copy = pltpu.make_async_copy(src, dst, store_sem.at[len(stores)])
        copy.start()
        stores.append(copy)

    for c in range(chunk_count):
        body = pl.ds(HALO, depth)
        store(field.at[(steps - 1) % 2, c, body, inner, :], earlier_out.at[:, :, lanes(c)])
        store(field.at[steps % 2, c, body, inner, :], latest_out.at[:, :, lanes(c)])
        store(light.at[c], light_out.at[:, :, lanes(c)])

    source = [source_ref[i].astype(jnp.float32) for i in range(3)]
    second_at = lax.broadcasted_iota(jnp.int32, (rows, LANES), 0).astype(jnp.float32) - source[1]
    third_at = lax.broadcasted_iota(jnp.int32, (rows, LANES), 1).astype(jnp.float32) - source[2]

    def mute(x, carry):
        first_at = (sub * depth + x).astype(jnp.float32) - source[0]
        base = first_at * first_at + second_at * second_at
        for c in range(chunk_count):
            along = third_at + float(c * LANES)
            distance = base + along * along
            image[c, x] = image[c, x] * (1.0 - jnp.exp(-distance / (2.0 * MUTE * MUTE)))
        return carry

    lax.fori_loop(0, depth, mute, 0)
    for c in range(chunk_count):
        store(image.at[c], image_out.at[:, :, lanes(c)])
    for copy in stores:
        copy.wait()


def local(
    stiffness, buoyancy_first, buoyancy_second, buoyancy_third, adjoint_before,
    adjoint_current, forward_field, traces, receiver_target, receiver_cell, source_cell,
):
    device_count = lax.axis_size(("shot", "sub"))
    sample_count = traces.shape[1]
    steps = forward_field.shape[1]
    depth, rows, length = stiffness.shape
    chunk_count = length // LANES
    row_count = traces.shape[0]
    capacity = max(2, (3 * row_count + 2 * device_count - 1) // (2 * device_count))
    slots = device_count * capacity

    kernel = trace_kernel(sample_count, steps)
    values = jnp.dot(
        traces, kernel, precision=lax.Precision.HIGHEST, preferred_element_type=jnp.float32)
    target = receiver_target[:, 0]
    onehot = target[:, None] == jnp.arange(device_count, dtype=jnp.int32)[None, :]
    row_ids = jnp.arange(row_count, dtype=jnp.int32)
    lower = (row_ids[:, None] >= row_ids[None, :]).astype(jnp.bfloat16)
    running = jnp.dot(lower, onehot.astype(jnp.bfloat16), preferred_element_type=jnp.float32)
    slot = (jnp.sum(jnp.where(onehot, running, 0.0), axis=1) - 1.0).astype(jnp.int32)
    chosen = (
        (target * capacity + slot)[None, :] == jnp.arange(slots, dtype=jnp.int32)[:, None]
    ).astype(jnp.float32)
    rows_out = jnp.concatenate([values, receiver_cell.astype(jnp.float32)[:, None]], axis=1)
    packed = jnp.dot(
        chosen, rows_out, precision=lax.Precision.HIGHEST, preferred_element_type=jnp.float32)
    got = lax.all_to_all(
        packed.reshape(device_count, capacity * (steps + 1)), ("shot", "sub"),
        split_axis=0, concat_axis=0, tiled=True).reshape(slots, steps + 1)
    groups = -(-slots // LANES)
    got = jnp.pad(got, ((0, groups * LANES - slots), (0, 0)))
    places = (got[:, steps] + 0.5).astype(jnp.int32)
    tiles = got[:, :steps].T.reshape(steps, groups, LANES).transpose(1, 0, 2)

    dense = pl.pallas_call(
        functools.partial(scatter_body, chunk_count, depth * rows),
        out_shape=jax.ShapeDtypeStruct((chunk_count * depth * rows, steps, LANES), jnp.float32),
        in_specs=[pl.BlockSpec(memory_space=pltpu.SMEM), pl.BlockSpec(memory_space=pltpu.VMEM)],
        out_specs=pl.BlockSpec(memory_space=pltpu.VMEM),
        compiler_params=pltpu.CompilerParams(vmem_limit_bytes=32 * 2**20),
    )(places, tiles).reshape(chunk_count, depth, rows * steps, LANES)

    f32 = jnp.float32
    grid_shape = jax.ShapeDtypeStruct((depth, rows, length), f32)
    anywhere = pl.BlockSpec(memory_space=pl.ANY)
    cells = (chunk_count, depth, rows, LANES)
    image, light, earlier, latest = pl.pallas_call(
        functools.partial(wave_body, (steps, depth, rows, chunk_count)),
        out_shape=[grid_shape] * 4,
        in_specs=[anywhere] * 8 + [pl.BlockSpec(memory_space=pltpu.SMEM)],
        out_specs=[anywhere] * 4,
        scratch_shapes=[
            pltpu.VMEM((2, chunk_count, depth + 2 * HALO, rows + 2 * PAD, LANES), f32),
            pltpu.VMEM(cells, f32),
            pltpu.VMEM((chunk_count, depth + 7, rows, LANES), f32),
            pltpu.VMEM(cells, f32),
            pltpu.VMEM(cells, f32),
            pltpu.VMEM(cells, f32),
            pltpu.VMEM(cells, f32),
            pltpu.VMEM(cells, f32),
            pltpu.VMEM((steps, depth, rows, length), jnp.bfloat16),
            pltpu.VMEM((chunk_count, depth, rows * steps, LANES), f32),
            pltpu.VMEM((chunk_count, rows + 2 * PAD, LANES), f32),
            pltpu.SemaphoreType.DMA((6 * chunk_count + 2,)),
            pltpu.SemaphoreType.DMA((4 * chunk_count,)),
            pltpu.SemaphoreType.DMA((2, chunk_count, 2)),
            pltpu.SemaphoreType.DMA((2, chunk_count, 2)),
            pltpu.SemaphoreType.DMA((2, chunk_count)),
            pltpu.SemaphoreType.DMA((2, chunk_count)),
        ],
        compiler_params=pltpu.CompilerParams(
            collective_id=0, has_side_effects=True, vmem_limit_bytes=48 * 2**20),
    )(
        stiffness, buoyancy_first, buoyancy_second, buoyancy_third, adjoint_before[0],
        adjoint_current[0], forward_field[0], dense, source_cell[0],
    )
    summed_image = lax.psum_scatter(image.reshape(depth, -1), "shot", scatter_dimension=1, tiled=True)
    summed_light = lax.psum_scatter(light.reshape(depth, -1), "shot", scatter_dimension=1, tiled=True)
    gradient = summed_image / (summed_light / (steps * lax.axis_size("shot")) + DAMP)
    return (gradient, earlier[None], latest[None])


def solution(mesh):
    placed = (
        P("sub", None, None),
        P("sub", None, None),
        P("sub", None, None),
        P("sub", None, None),
        P("shot", "sub", None, None),
        P("shot", "sub", None, None),
        P("shot", None, "sub", None, None),
        P(("shot", "sub"), None),
        P(("shot", "sub"), None),
        P(("shot", "sub")),
        P("shot", None),
    )
    return jax.shard_map(
        local,
        mesh=mesh,
        in_specs=placed,
        out_specs=(P("sub", "shot"), P("shot", "sub", None, None), P("shot", "sub", None, None)),
        check_vma=False,
    )
```

```python
import functools

import jax
import jax.numpy as jnp
from jax import lax
from jax.experimental import pallas as pl
from jax.experimental.pallas import tpu as pltpu
from jax.sharding import PartitionSpec as P

MUTE = 6
COEFFS = (1225.0 / 1024.0, -245.0 / 3072.0, 49.0 / 5120.0, -5.0 / 7168.0)
RATIOS = tuple(c / COEFFS[0] for c in COEFFS)
SCALE = COEFFS[0] * COEFFS[0]
DAMP = 0.1
LANES = 128
HALO = 7
PAD = 8
MESH = pl.DeviceIdType.MESH


def trace_kernel(sample_count, step_count):
    sample_pos = jnp.arange(sample_count, dtype=jnp.float32)[:, None]
    centers = (jnp.arange(step_count, dtype=jnp.float32)[None, :] + 0.5) * (
        sample_count / step_count
    )
    return 0.25 * jnp.exp(-jnp.abs(sample_pos - centers) / (sample_count / 8.0))


def weighted(pairs):
    total = pairs[0][0] - pairs[0][1]
    for ratio, (ahead, behind) in zip(RATIOS[1:], pairs[1:]):
        total = total + ratio * (ahead - behind)
    return total


def shifted(chunks, amount, lane):
    if amount == 0:
        return chunks
    rolled = [pltpu.roll(chunk, (-amount) % LANES, 1) for chunk in chunks]
    zero = jnp.zeros_like(chunks[0])
    out = []
    for c in range(len(chunks)):
        if amount > 0:
            other = rolled[c + 1] if c + 1 < len(chunks) else zero
            out.append(jnp.where(lane < LANES - amount, rolled[c], other))
        else:
            other = rolled[c - 1] if c > 0 else zero
            out.append(jnp.where(lane >= -amount, rolled[c], other))
    return out


def scatter_body(row_ref, at_ref, turn_ref, value_ref, dense_ref):
    dense_ref[...] = jnp.zeros_like(dense_ref)
    lane = lax.broadcasted_iota(jnp.int32, (8, LANES), 1)

    def block(group, carry):
        tile = value_ref[group]

        def one(slot, inner):
            number = group * LANES + slot
            row = row_ref[number]
            moved = pltpu.roll(tile, turn_ref[number], 1)
            dense_ref[row] = dense_ref[row] + jnp.where(lane == at_ref[number], moved, 0.0)
            return inner

        return lax.fori_loop(0, LANES, one, carry, unroll=8)

    lax.fori_loop(0, value_ref.shape[0], block, 0)


def wave_body(
    dims,
    stiff_hbm, first_hbm, second_hbm, third_hbm, before_hbm, current_hbm, forward_hbm,
    inject_hbm, source_ref,
    gradient_out, earlier_out, latest_out,
    field, stiff, first, second, third, partial, image, forward, inject, flux,
    light_blocks, light_got, image_blocks, image_got, image_last,
    load_sem, store_sem, edge_send, edge_recv, face_send, face_recv,
    light_send, light_recv, across_send, across_recv, along_send, along_recv,
):
    steps, depth, rows, chunk_count, lines, columns = dims
    shots = lines * columns
    share = rows // shots
    shot = lax.axis_index("shot")
    line, column = lax.div(shot, columns), lax.rem(shot, columns)
    sub = lax.axis_index("sub")
    ends = lax.axis_size("sub") - 1
    has_left = sub > 0
    has_right = sub < ends
    zero_tile = jnp.zeros((8, LANES), jnp.float32)

    for c in range(chunk_count):
        def clear(plane, carry, c=c):
            for b in range(2):
                field[b, c, plane, 0:PAD, :] = zero_tile
                field[b, c, plane, PAD + rows:2 * PAD + rows, :] = zero_tile
            return carry
        lax.fori_loop(HALO, HALO + depth, clear, 0)
        for plane in list(range(HALO)) + list(range(HALO + depth, 2 * HALO + depth)):
            for b in range(2):
                field[b, c, plane] = jnp.zeros((2 * PAD + rows, LANES), jnp.float32)
        for face in list(range(4)) + list(range(4 + depth, 7 + depth)):
            first[c, face] = jnp.zeros((rows, LANES), jnp.float32)
        flux[c] = jnp.zeros((2 * PAD + rows, LANES), jnp.float32)

    barrier = pltpu.get_barrier_semaphore()

    @pl.when(has_left)
    def _():
        pl.semaphore_signal(barrier, inc=1, device_id={"sub": sub - 1}, device_id_type=MESH)

    @pl.when(has_right)
    def _():
        pl.semaphore_signal(barrier, inc=1, device_id={"sub": sub + 1}, device_id_type=MESH)

    for k in range(1, shots):
        pl.semaphore_signal(
            barrier, inc=1, device_id={"shot": lax.rem(shot + k, shots)}, device_id_type=MESH)

    def lanes(c):
        return pl.ds(c * LANES, LANES)

    inner = pl.ds(PAD, rows)
    loads = []

    def load(src, dst):
        copy = pltpu.make_async_copy(src, dst, load_sem.at[len(loads)])
        copy.start()
        loads.append(copy)

    for c in range(chunk_count):
        load(current_hbm.at[:, :, lanes(c)], field.at[0, c, pl.ds(HALO, depth), inner, :])
        load(third_hbm.at[:, :, lanes(c)], third.at[c])
        load(second_hbm.at[:, :, lanes(c)], second.at[c])
    early = len(loads)
    load(forward_hbm, forward)
    for c in range(chunk_count):
        load(first_hbm.at[:, :, lanes(c)], first.at[c, pl.ds(4, depth)])
        load(stiff_hbm.at[:, :, lanes(c)], stiff.at[c])
        load(before_hbm.at[:, :, lanes(c)], field.at[1, c, pl.ds(HALO, depth), inner, :])
    load(inject_hbm, inject)

    pl.semaphore_wait(
        barrier, (shots - 1) + jnp.where(has_left, 1, 0) + jnp.where(has_right, 1, 0))

    def face_copy(side, c):
        if side == 0:
            src = first_hbm.at[pl.ds(0, 3), :, lanes(c)]
            dst = first.at[c, pl.ds(4 + depth, 3)]
            to = sub - 1
        else:
            src = first_hbm.at[pl.ds(depth - 4, 4), :, lanes(c)]
            dst = first.at[c, pl.ds(0, 4)]
            to = sub + 1
        return pltpu.make_async_remote_copy(
            src, dst, face_send.at[side, c], face_recv.at[side, c],
            device_id={"sub": to}, device_id_type=MESH)

    def edge_copy(side, c, b, from_hbm=False):
        start = 0 if side == 0 else depth - HALO
        if from_hbm:
            src = current_hbm.at[pl.ds(start, HALO), :, lanes(c)]
        else:
            src = field.at[b, c, pl.ds(HALO + start, HALO), inner, :]
        dst = field.at[b, c, pl.ds(HALO + depth if side == 0 else 0, HALO), inner, :]
        return pltpu.make_async_remote_copy(
            src, dst, edge_send.at[side, c, b], edge_recv.at[side, c, b],
            device_id={"sub": sub - 1 if side == 0 else sub + 1}, device_id_type=MESH)

    sends_on = (has_left, has_right)
    gets_on = (has_right, has_left)
    for c in range(chunk_count):
        for side in range(2):
            @pl.when(sends_on[side])
            def _(side=side, c=c):
                edge_copy(side, c, 0, True).start()
                face_copy(side, c).start()

    lane = lax.broadcasted_iota(jnp.int32, (8, LANES), 1)
    base = PAD + lax.div(sub, lax.axis_size("sub"))
    for copy in loads[:early]:
        copy.wait()

    def inner_part(b, x, carry):
        for y in range(0, rows, 8):
            at = pl.ds(y, 8)
            p = [field[b, c, HALO + x, pl.ds(PAD + y, 8), :] for c in range(chunk_count)]
            pairs = [(shifted(p, k, lane), shifted(p, 1 - k, lane)) for k in range(1, 5)]
            q = [
                third[c, x, at, :] * weighted([(a[c], z[c]) for a, z in pairs])
                for c in range(chunk_count)
            ]
            pairs = [(shifted(q, k - 1, lane), shifted(q, -k, lane)) for k in range(1, 5)]
            for c in range(chunk_count):
                partial[c, x, at, :] = weighted([(a[c], z[c]) for a, z in pairs])
        for c in range(chunk_count):
            for y in range(0, rows, 8):
                def near(s, c=c, y=y):
                    return field[b, c, HALO + x, pl.ds(base + (y + s), 8), :]
                flux[c, pl.ds(PAD + y, 8), :] = second[c, x, pl.ds(y, 8), :] * weighted(
                    [(near(k), near(1 - k)) for k in range(1, 5)])
        for c in range(chunk_count):
            for y in range(0, rows, 8):
                def near(s, c=c, y=y):
                    return flux[c, pl.ds(base + (y + s), 8), :]
                at = pl.ds(y, 8)
                partial[c, x, at, :] = partial[c, x, at, :] + weighted(
                    [(near(k - 1), near(-k)) for k in range(1, 5)])
        return carry

    def inner_all(b):
        lax.fori_loop(0, depth, functools.partial(inner_part, b), 0)

    inner_all(0)
    for copy in loads[early:]:
        copy.wait()

    def put_blocks(blocks, c, x, value):
        for d in range(shots):
            blocks[d % columns, c, d // columns, pl.ds(x * share, share), :] = (
                value[d * share:(d + 1) * share, :])

    def prepare(x, carry):
        for c in range(chunk_count):
            stiff[c, x] = stiff[c, x] * SCALE
            total = jnp.zeros((rows, LANES), jnp.float32)
            for t in range(steps):
                frame = forward[t, x, :, c * LANES:(c + 1) * LANES].astype(jnp.float32)
                total = total + frame * frame
            put_blocks(light_blocks, c, x, total)
            image[c, x] = jnp.zeros((rows, LANES), jnp.float32)
        return carry

    lax.fori_loop(0, depth, prepare, 0)

    def light_copy(k):
        to = lax.rem(shot + k, shots)
        return pltpu.make_async_remote_copy(
            light_blocks.at[lax.rem(to, columns), :, lax.div(to, columns)],
            light_got.at[k - 1], light_send.at[k - 1], light_recv.at[k - 1],
            device_id={"shot": to}, device_id_type=MESH)

    for k in range(1, shots):
        light_copy(k).start()

    def across_copy(k, c):
        to = lax.rem(column + k, columns)
        return pltpu.make_async_remote_copy(
            image_blocks.at[to, c], image_got.at[k - 1, c],
            across_send.at[k - 1, c], across_recv.at[k - 1, c],
            device_id={"shot": line * columns + to}, device_id_type=MESH)

    def along_copy(k, c):
        to = lax.rem(line + k, lines)
        return pltpu.make_async_remote_copy(
            image_blocks.at[column, c, to], image_last.at[k - 1, c],
            along_send.at[k - 1, c], along_recv.at[k - 1, c],
            device_id={"shot": to * columns + column}, device_id_type=MESH)

    source = [source_ref[i].astype(jnp.float32) for i in range(3)]
    second_at = lax.broadcasted_iota(jnp.int32, (rows, LANES), 0).astype(jnp.float32) - source[1]
    third_at = lax.broadcasted_iota(jnp.int32, (rows, LANES), 1).astype(jnp.float32) - source[2]

    def mute(c, x, carry):
        first_at = (sub * depth + x).astype(jnp.float32) - source[0]
        along = third_at + float(c * LANES)
        distance = first_at * first_at + second_at * second_at + along * along
        put_blocks(
            image_blocks, c, x, image[c, x] * (1.0 - jnp.exp(-distance / (2.0 * MUTE * MUTE))))
        return carry

    for c in range(chunk_count):
        for side in range(2):
            @pl.when(gets_on[side])
            def _(side=side, c=c):
                face_copy(side, c).wait_recv()

            @pl.when(sends_on[side])
            def _(side=side, c=c):
                face_copy(side, c).wait_send()

    def outer_part(c, t, b, half, carry):
        y = pl.multiple_of(half * 16, 16)
        at = pl.ds(y, 16)
        wide = pl.ds(pl.multiple_of(PAD + y, 8), 16)
        p = [field[b, c, i, wide, :] for i in range(8)]
        q = []
        for f in range(-4, depth + 3):
            q.append(first[c, f + 4, at, :] * weighted([(p[3 + k], p[4 - k]) for k in range(1, 5)]))
            x = f - 3
            if x >= 0:
                div = weighted([(q[3 + k], q[4 - k]) for k in range(1, 5)]) + partial[c, x, at, :]
                change = stiff[c, x, at, :] * div + inject[c, x, pl.ds(t + 8 * y, 16, stride=8), :]
                now = p[0]
                past = field[1 - b, c, HALO + x, wide, :]
                field[1 - b, c, HALO + x, wide, :] = (now + now) - past + change
                frame = forward[t, x, at, c * LANES:(c + 1) * LANES].astype(jnp.float32)
                image[c, x, at, :] = image[c, x, at, :] + frame * change
                q = q[1:]
            if f + 1 < depth + 3:
                p = p[1:] + [field[b, c, f + 5 + HALO, wide, :]]
        return carry

    def one_step(t, carry):
        b = lax.rem(t, 2)

        @pl.when(t > 0)
        def _():
            inner_all(b)

        for c in range(chunk_count):
            for side in range(2):
                @pl.when(gets_on[side])
                def _(side=side, c=c):
                    edge_copy(side, c, b).wait_recv()

                @pl.when(sends_on[side])
                def _(side=side, c=c):
                    edge_copy(side, c, b).wait_send()

            lax.fori_loop(0, rows // 16, functools.partial(outer_part, c, t, b), 0)
            for side in range(2):
                @pl.when(jnp.logical_and(sends_on[side], t < steps - 1))
                def _(side=side, c=c):
                    edge_copy(side, c, 1 - b).start()

            @pl.when(t == steps - 1)
            def _(c=c):
                lax.fori_loop(0, depth, functools.partial(mute, c), 0)
                for k in range(1, columns):
                    across_copy(k, c).start()
        return carry

    lax.fori_loop(0, steps, one_step, 0)

    stores = []

    def store(src, dst):
        copy = pltpu.make_async_copy(src, dst, store_sem.at[len(stores)])
        copy.start()
        stores.append(copy)

    for c in range(chunk_count):
        body = pl.ds(HALO, depth)
        store(field.at[(steps - 1) % 2, c, body, inner, :], earlier_out.at[:, :, lanes(c)])
        store(field.at[steps % 2, c, body, inner, :], latest_out.at[:, :, lanes(c)])

    for c in range(chunk_count):
        for k in range(1, columns):
            across_copy(k, c).wait()
            image_blocks[column, c] = image_blocks[column, c] + image_got[k - 1, c]
        for k in range(1, lines):
            along_copy(k, c).start()
    for k in range(1, shots):
        light_copy(k).wait()
    for c in range(chunk_count):
        light = light_blocks[column, c, line]
        for k in range(1, shots):
            light = light + light_got[k - 1, c]
        summed = image_blocks[column, c, line]
        for k in range(1, lines):
            along_copy(k, c).wait()
            summed = summed + image_last[k - 1, c]
        gradient_out[c] = summed / (light / (steps * shots) + DAMP)
    for copy in stores:
        copy.wait()


def local(
    stiffness, buoyancy_first, buoyancy_second, buoyancy_third, adjoint_before,
    adjoint_current, forward_field, traces, receiver_target, receiver_cell, source_cell,
):
    device_count = lax.axis_size(("shot", "sub"))
    sample_count = traces.shape[1]
    steps = forward_field.shape[1]
    depth, rows, length = stiffness.shape
    chunk_count = length // LANES
    row_count = traces.shape[0]
    capacity = max(2, (3 * row_count + 2 * device_count - 1) // (2 * device_count))
    slots = device_count * capacity

    kernel = trace_kernel(sample_count, steps)
    values = jnp.dot(
        traces, kernel, precision=lax.Precision.HIGHEST, preferred_element_type=jnp.float32)
    target = receiver_target[:, 0]
    onehot = target[:, None] == jnp.arange(device_count, dtype=jnp.int32)[None, :]
    row_ids = jnp.arange(row_count, dtype=jnp.int32)
    lower = (row_ids[:, None] >= row_ids[None, :]).astype(jnp.bfloat16)
    running = jnp.dot(lower, onehot.astype(jnp.bfloat16), preferred_element_type=jnp.float32)
    slot = (jnp.sum(jnp.where(onehot, running, 0.0), axis=1) - 1.0).astype(jnp.int32)
    chosen = (
        (target * capacity + slot)[None, :] == jnp.arange(slots, dtype=jnp.int32)[:, None]
    ).astype(jnp.float32)
    rows_out = jnp.concatenate([values, receiver_cell.astype(jnp.float32)[:, None]], axis=1)
    packed = jnp.dot(
        chosen, rows_out, precision=lax.Precision.HIGHEST, preferred_element_type=jnp.float32)
    got = lax.all_to_all(
        packed.reshape(device_count, capacity * (steps + 1)), ("shot", "sub"),
        split_axis=0, concat_axis=0, tiled=True).reshape(slots, steps + 1)
    groups = -(-slots // LANES)
    got = jnp.pad(got, ((0, groups * LANES - slots), (0, 0)))
    places = (got[:, steps] + 0.5).astype(jnp.int32)
    spots = places // LANES
    spot_rows = (spots % chunk_count) * (depth * rows) + spots // chunk_count
    lane_at = places % LANES
    turns = (lane_at - jnp.arange(groups * LANES, dtype=jnp.int32)) % LANES
    tiles = got[:, :steps].T.reshape(steps, groups, LANES).transpose(1, 0, 2)

    dense = pl.pallas_call(
        scatter_body,
        out_shape=jax.ShapeDtypeStruct((chunk_count * depth * rows, steps, LANES), jnp.float32),
        in_specs=[pl.BlockSpec(memory_space=pltpu.SMEM)] * 3
        + [pl.BlockSpec(memory_space=pltpu.VMEM)],
        out_specs=pl.BlockSpec(memory_space=pltpu.VMEM),
        compiler_params=pltpu.CompilerParams(vmem_limit_bytes=32 * 2**20),
    )(spot_rows, lane_at, turns, tiles).reshape(chunk_count, depth, rows * steps, LANES)

    f32 = jnp.float32
    grid_shape = jax.ShapeDtypeStruct((depth, rows, length), f32)
    anywhere = pl.BlockSpec(memory_space=pl.ANY)
    cells = (chunk_count, depth, rows, LANES)
    shots = lax.axis_size("shot")
    lines = 4 if shots % 4 == 0 else 1
    columns = shots // lines
    part = depth * (rows // shots)
    shares = (columns, chunk_count, lines, part, LANES)
    dma = pltpu.SemaphoreType.DMA
    gradient, earlier, latest = pl.pallas_call(
        functools.partial(wave_body, (steps, depth, rows, chunk_count, lines, columns)),
        out_shape=[jax.ShapeDtypeStruct((chunk_count, part, LANES), f32)] + [grid_shape] * 2,
        in_specs=[anywhere] * 8 + [pl.BlockSpec(memory_space=pltpu.SMEM)],
        out_specs=[pl.BlockSpec(memory_space=pltpu.VMEM)] + [anywhere] * 2,
        scratch_shapes=[
            pltpu.VMEM((2, chunk_count, depth + 2 * HALO, rows + 2 * PAD, LANES), f32),
            pltpu.VMEM(cells, f32),
            pltpu.VMEM((chunk_count, depth + 7, rows, LANES), f32),
            pltpu.VMEM(cells, f32),
            pltpu.VMEM(cells, f32),
            pltpu.VMEM(cells, f32),
            pltpu.VMEM(cells, f32),
            pltpu.VMEM((steps, depth, rows, length), jnp.bfloat16),
            pltpu.VMEM((chunk_count, depth, rows * steps, LANES), f32),
            pltpu.VMEM((chunk_count, rows + 2 * PAD, LANES), f32),
            pltpu.VMEM(shares, f32),
            pltpu.VMEM((shots - 1, chunk_count, part, LANES), f32),
            pltpu.VMEM(shares, f32),
            pltpu.VMEM((max(1, columns - 1),) + shares[1:], f32),
            pltpu.VMEM((max(1, lines - 1), chunk_count, part, LANES), f32),
            dma((6 * chunk_count + 2,)),
            dma((2 * chunk_count,)),
            dma((2, chunk_count, 2)),
            dma((2, chunk_count, 2)),
            dma((2, chunk_count)),
            dma((2, chunk_count)),
            dma((shots - 1,)),
            dma((shots - 1,)),
            dma((max(1, columns - 1), chunk_count)),
            dma((max(1, columns - 1), chunk_count)),
            dma((max(1, lines - 1), chunk_count)),
            dma((max(1, lines - 1), chunk_count)),
        ],
        compiler_params=pltpu.CompilerParams(
            collective_id=0, has_side_effects=True, vmem_limit_bytes=48 * 2**20),
    )(
        stiffness, buoyancy_first, buoyancy_second, buoyancy_third, adjoint_before[0],
        adjoint_current[0], forward_field[0], dense, source_cell[0],
    )
    gradient = gradient.reshape(chunk_count, depth, rows // shots, LANES)
    gradient = gradient.transpose(1, 2, 0, 3).reshape(depth, -1)
    return (gradient, earlier[None], latest[None])


def solution(mesh):
    placed = (
        P("sub", None, None),
        P("sub", None, None),
        P("sub", None, None),
        P("sub", None, None),
        P("shot", "sub", None, None),
        P("shot", "sub", None, None),
        P("shot", None, "sub", None, None),
        P(("shot", "sub"), None),
        P(("shot", "sub"), None),
        P(("shot", "sub")),
        P("shot", None),
    )
    return jax.shard_map(
        local,
        mesh=mesh,
        in_specs=placed,
        out_specs=(P("sub", "shot"), P("shot", "sub", None, None), P("shot", "sub", None, None)),
        check_vma=False,
    )
```

```python
import functools

import jax
import jax.numpy as jnp
from jax import lax
from jax.experimental import pallas as pl
from jax.experimental.pallas import tpu as pltpu
from jax.sharding import PartitionSpec as P

MUTE = 6
COEFFS = (1225.0 / 1024.0, -245.0 / 3072.0, 49.0 / 5120.0, -5.0 / 7168.0)
RATIOS = tuple(c / COEFFS[0] for c in COEFFS)
SCALE = COEFFS[0] * COEFFS[0]
DAMP = 0.1
LANES = 128
HALO = 7
PAD = 8
MESH = pl.DeviceIdType.MESH


def trace_kernel(sample_count, step_count):
    sample_pos = jnp.arange(sample_count, dtype=jnp.float32)[:, None]
    centers = (jnp.arange(step_count, dtype=jnp.float32)[None, :] + 0.5) * (
        sample_count / step_count
    )
    return 0.25 * jnp.exp(-jnp.abs(sample_pos - centers) / (sample_count / 8.0))


def weighted(pairs):
    total = pairs[0][0] - pairs[0][1]
    for ratio, (ahead, behind) in zip(RATIOS[1:], pairs[1:]):
        total = total + ratio * (ahead - behind)
    return total


def shifted(chunks, amount, lane):
    if amount == 0:
        return chunks
    rolled = [pltpu.roll(chunk, (-amount) % LANES, 1) for chunk in chunks]
    zero = jnp.zeros_like(chunks[0])
    out = []
    for c in range(len(chunks)):
        if amount > 0:
            other = rolled[c + 1] if c + 1 < len(chunks) else zero
            out.append(jnp.where(lane < LANES - amount, rolled[c], other))
        else:
            other = rolled[c - 1] if c > 0 else zero
            out.append(jnp.where(lane >= -amount, rolled[c], other))
    return out


def exchange_body(shots, subs, mine_ref, got_ref, send_sem, recv_sem):
    count = shots * subs
    me = lax.axis_index("shot") * subs + lax.axis_index("sub")

    def place(k):
        to = lax.rem(me + k, count)
        return {"shot": lax.div(to, subs), "sub": lax.rem(to, subs)}, to

    barrier = pltpu.get_barrier_semaphore()

    def greet(k, carry):
        pl.semaphore_signal(barrier, inc=1, device_id=place(k)[0], device_id_type=MESH)
        return carry

    lax.fori_loop(1, count, greet, 0)
    got_ref[count - 1] = mine_ref[me]
    pl.semaphore_wait(barrier, count - 1)

    def copy(k):
        device, to = place(k)
        return pltpu.make_async_remote_copy(
            mine_ref.at[to], got_ref.at[k - 1], send_sem.at[k - 1], recv_sem.at[k - 1],
            device_id=device, device_id_type=MESH)

    def send(k, carry):
        copy(k).start()
        return carry

    def finish(k, carry):
        copy(k).wait()
        return carry

    lax.fori_loop(1, count, send, 0)
    lax.fori_loop(1, count, finish, 0)


def scatter_body(row_ref, at_ref, turn_ref, value_ref, dense_ref):
    dense_ref[...] = jnp.zeros_like(dense_ref)
    lane = lax.broadcasted_iota(jnp.int32, (8, LANES), 1)

    def block(group, carry):
        tile = value_ref[group]

        def four(quad, inner):
            spots, terms, found = [], [], []
            for k in range(4):
                number = group * LANES + quad * 4 + k
                spots.append(row_ref[number])
                moved = pltpu.roll(tile, turn_ref[number], 1)
                terms.append(jnp.where(lane == at_ref[number], moved, 0.0))
                found.append(dense_ref[spots[k]])
            for k in range(4):
                total = found[k] + terms[k]
                for before in range(k):
                    same = jnp.where(spots[before] == spots[k], 1.0, 0.0)
                    total = total + terms[before] * same
                dense_ref[spots[k]] = total
            return inner

        return lax.fori_loop(0, LANES // 4, four, carry, unroll=4)

    lax.fori_loop(0, value_ref.shape[0], block, 0)


def wave_body(
    dims,
    stiff_hbm, first_hbm, second_hbm, third_hbm, before_hbm, current_hbm, forward_hbm,
    left_hbm, right_hbm, inject, source_ref,
    gradient_out, earlier_out, latest_out,
    field, stiff, first, second, third, partial, image, forward, flux,
    light_blocks, light_got, image_blocks, image_got, image_last,
    load_sem, store_sem, edge_send, edge_recv,
    light_send, light_recv, across_send, across_recv, along_send, along_recv,
):
    steps, depth, rows, chunk_count, lines, columns = dims
    shots = lines * columns
    share = rows // shots
    shot = lax.axis_index("shot")
    line, column = lax.div(shot, columns), lax.rem(shot, columns)
    sub = lax.axis_index("sub")
    ends = lax.axis_size("sub") - 1
    has_left = sub > 0
    has_right = sub < ends
    zero_tile = jnp.zeros((8, LANES), jnp.float32)

    for c in range(chunk_count):
        def clear(plane, carry, c=c):
            for b in range(2):
                field[b, c, plane, 0:PAD, :] = zero_tile
                field[b, c, plane, PAD + rows:2 * PAD + rows, :] = zero_tile
            return carry
        lax.fori_loop(HALO, HALO + depth, clear, 0)
        for plane in list(range(HALO)) + list(range(HALO + depth, 2 * HALO + depth)):
            for b in range(2):
                field[b, c, plane] = jnp.zeros((2 * PAD + rows, LANES), jnp.float32)
        flux[c] = jnp.zeros((2 * PAD + rows, LANES), jnp.float32)

    barrier = pltpu.get_barrier_semaphore()

    @pl.when(has_left)
    def _():
        pl.semaphore_signal(barrier, inc=1, device_id={"sub": sub - 1}, device_id_type=MESH)

    @pl.when(has_right)
    def _():
        pl.semaphore_signal(barrier, inc=1, device_id={"sub": sub + 1}, device_id_type=MESH)

    for k in range(1, shots):
        pl.semaphore_signal(
            barrier, inc=1, device_id={"shot": lax.rem(shot + k, shots)}, device_id_type=MESH)

    def lanes(c):
        return pl.ds(c * LANES, LANES)

    inner = pl.ds(PAD, rows)
    loads = []

    def load(src, dst):
        copy = pltpu.make_async_copy(src, dst, load_sem.at[len(loads)])
        copy.start()
        loads.append(copy)

    for c in range(chunk_count):
        load(current_hbm.at[:, :, lanes(c)], field.at[0, c, pl.ds(HALO, depth), inner, :])
        load(third_hbm.at[:, :, lanes(c)], third.at[c])
        load(second_hbm.at[:, :, lanes(c)], second.at[c])
    early = len(loads)
    load(forward_hbm, forward)
    for c in range(chunk_count):
        load(first_hbm.at[:, :, lanes(c)], first.at[c, pl.ds(4, depth)])
        load(stiff_hbm.at[:, :, lanes(c)], stiff.at[c])
        load(before_hbm.at[:, :, lanes(c)], field.at[1, c, pl.ds(HALO, depth), inner, :])
    for c in range(chunk_count):
        load(left_hbm.at[pl.ds(0, HALO), :, lanes(c)], field.at[0, c, pl.ds(0, HALO), inner, :])
        load(left_hbm.at[pl.ds(HALO, 4), :, lanes(c)], first.at[c, pl.ds(0, 4)])
        load(right_hbm.at[pl.ds(0, HALO), :, lanes(c)],
             field.at[0, c, pl.ds(HALO + depth, HALO), inner, :])
        load(right_hbm.at[pl.ds(HALO, 3), :, lanes(c)], first.at[c, pl.ds(4 + depth, 3)])

    pl.semaphore_wait(
        barrier, (shots - 1) + jnp.where(has_left, 1, 0) + jnp.where(has_right, 1, 0))

    def edge_copy(side, c, b):
        start = 0 if side == 0 else depth - HALO
        src = field.at[b, c, pl.ds(HALO + start, HALO), inner, :]
        dst = field.at[b, c, pl.ds(HALO + depth if side == 0 else 0, HALO), inner, :]
        return pltpu.make_async_remote_copy(
            src, dst, edge_send.at[side, c, b], edge_recv.at[side, c, b],
            device_id={"sub": sub - 1 if side == 0 else sub + 1}, device_id_type=MESH)

    sends_on = (has_left, has_right)
    gets_on = (has_right, has_left)
    lane = lax.broadcasted_iota(jnp.int32, (8, LANES), 1)
    base = PAD + lax.div(sub, lax.axis_size("sub"))
    for copy in loads[:early]:
        copy.wait()

    def inner_part(b, x, carry):
        for y in range(0, rows, 8):
            at = pl.ds(y, 8)
            p = [field[b, c, HALO + x, pl.ds(PAD + y, 8), :] for c in range(chunk_count)]
            pairs = [(shifted(p, k, lane), shifted(p, 1 - k, lane)) for k in range(1, 5)]
            q = [
                third[c, x, at, :] * weighted([(a[c], z[c]) for a, z in pairs])
                for c in range(chunk_count)
            ]
            pairs = [(shifted(q, k - 1, lane), shifted(q, -k, lane)) for k in range(1, 5)]
            for c in range(chunk_count):
                partial[c, x, at, :] = weighted([(a[c], z[c]) for a, z in pairs])
        for c in range(chunk_count):
            for y in range(0, rows, 8):
                def near(s, c=c, y=y):
                    return field[b, c, HALO + x, pl.ds(base + (y + s), 8), :]
                flux[c, pl.ds(PAD + y, 8), :] = second[c, x, pl.ds(y, 8), :] * weighted(
                    [(near(k), near(1 - k)) for k in range(1, 5)])
        for c in range(chunk_count):
            for y in range(0, rows, 8):
                def near(s, c=c, y=y):
                    return flux[c, pl.ds(base + (y + s), 8), :]
                at = pl.ds(y, 8)
                partial[c, x, at, :] = partial[c, x, at, :] + weighted(
                    [(near(k - 1), near(-k)) for k in range(1, 5)])
        return carry

    def inner_all(b):
        lax.fori_loop(0, depth, functools.partial(inner_part, b), 0)

    inner_all(0)
    for copy in loads[early:]:
        copy.wait()

    def put_blocks(blocks, c, x, value):
        for d in range(shots):
            blocks[d % columns, c, d // columns, pl.ds(x * share, share), :] = (
                value[d * share:(d + 1) * share, :])

    def prepare(x, carry):
        for c in range(chunk_count):
            stiff[c, x] = stiff[c, x] * SCALE
            total = jnp.zeros((rows, LANES), jnp.float32)
            for t in range(steps):
                frame = forward[t, x, :, c * LANES:(c + 1) * LANES].astype(jnp.float32)
                total = total + frame * frame
            put_blocks(light_blocks, c, x, total)
            image[c, x] = jnp.zeros((rows, LANES), jnp.float32)
        return carry

    lax.fori_loop(0, depth, prepare, 0)

    def light_copy(k):
        to = lax.rem(shot + k, shots)
        return pltpu.make_async_remote_copy(
            light_blocks.at[lax.rem(to, columns), :, lax.div(to, columns)],
            light_got.at[k - 1], light_send.at[k - 1], light_recv.at[k - 1],
            device_id={"shot": to}, device_id_type=MESH)

    for k in range(1, shots):
        light_copy(k).start()

    def across_copy(k, c):
        to = lax.rem(column + k, columns)
        return pltpu.make_async_remote_copy(
            image_blocks.at[to, c], image_got.at[k - 1, c],
            across_send.at[k - 1, c], across_recv.at[k - 1, c],
            device_id={"shot": line * columns + to}, device_id_type=MESH)

    def along_copy(k, c):
        to = lax.rem(line + k, lines)
        return pltpu.make_async_remote_copy(
            image_blocks.at[column, c, to], image_last.at[k - 1, c],
            along_send.at[k - 1, c], along_recv.at[k - 1, c],
            device_id={"shot": to * columns + column}, device_id_type=MESH)

    source = [source_ref[i].astype(jnp.float32) for i in range(3)]
    second_at = lax.broadcasted_iota(jnp.int32, (rows, LANES), 0).astype(jnp.float32) - source[1]
    third_at = lax.broadcasted_iota(jnp.int32, (rows, LANES), 1).astype(jnp.float32) - source[2]

    def mute(c, x, carry):
        first_at = (sub * depth + x).astype(jnp.float32) - source[0]
        along = third_at + float(c * LANES)
        distance = first_at * first_at + second_at * second_at + along * along
        put_blocks(
            image_blocks, c, x, image[c, x] * (1.0 - jnp.exp(-distance / (2.0 * MUTE * MUTE))))
        return carry

    def outer_part(c, t, b, half, carry):
        y = pl.multiple_of(half * 16, 16)
        at = pl.ds(y, 16)
        wide = pl.ds(pl.multiple_of(PAD + y, 8), 16)
        p = [field[b, c, i, wide, :] for i in range(8)]
        q = []
        for f in range(-4, depth + 3):
            q.append(first[c, f + 4, at, :] * weighted([(p[3 + k], p[4 - k]) for k in range(1, 5)]))
            x = f - 3
            if x >= 0:
                div = weighted([(q[3 + k], q[4 - k]) for k in range(1, 5)]) + partial[c, x, at, :]
                change = stiff[c, x, at, :] * div + inject[c, x, pl.ds(t + 8 * y, 16, stride=8), :]
                now = p[0]
                past = field[1 - b, c, HALO + x, wide, :]
                field[1 - b, c, HALO + x, wide, :] = (now + now) - past + change
                frame = forward[t, x, at, c * LANES:(c + 1) * LANES].astype(jnp.float32)
                image[c, x, at, :] = image[c, x, at, :] + frame * change
                q = q[1:]
            if f + 1 < depth + 3:
                p = p[1:] + [field[b, c, f + 5 + HALO, wide, :]]
        return carry

    def one_step(t, carry):
        b = lax.rem(t, 2)

        @pl.when(t > 0)
        def _():
            inner_all(b)

        for c in range(chunk_count):
            for side in range(2):
                @pl.when(jnp.logical_and(gets_on[side], t > 0))
                def _(side=side, c=c):
                    edge_copy(side, c, b).wait_recv()

                @pl.when(jnp.logical_and(sends_on[side], t > 0))
                def _(side=side, c=c):
                    edge_copy(side, c, b).wait_send()

            lax.fori_loop(0, rows // 16, functools.partial(outer_part, c, t, b), 0)
            for side in range(2):
                @pl.when(jnp.logical_and(sends_on[side], t < steps - 1))
                def _(side=side, c=c):
                    edge_copy(side, c, 1 - b).start()

            @pl.when(t == steps - 1)
            def _(c=c):
                lax.fori_loop(0, depth, functools.partial(mute, c), 0)
                for k in range(1, columns):
                    across_copy(k, c).start()
        return carry

    lax.fori_loop(0, steps, one_step, 0)

    stores = []

    def store(src, dst):
        copy = pltpu.make_async_copy(src, dst, store_sem.at[len(stores)])
        copy.start()
        stores.append(copy)

    for c in range(chunk_count):
        body = pl.ds(HALO, depth)
        store(field.at[(steps - 1) % 2, c, body, inner, :], earlier_out.at[:, :, lanes(c)])
        store(field.at[steps % 2, c, body, inner, :], latest_out.at[:, :, lanes(c)])

    for k in range(1, shots):
        light_copy(k).wait()
    for c in range(chunk_count):
        light = light_blocks[column, c, line]
        for k in range(1, shots):
            light = light + light_got[k - 1, c]
        light_blocks[column, c, line] = light / (steps * shots) + DAMP
    for c in range(chunk_count):
        for k in range(1, columns):
            across_copy(k, c).wait()
            image_blocks[column, c] = image_blocks[column, c] + image_got[k - 1, c]
        for k in range(1, lines):
            along_copy(k, c).start()
    for c in range(chunk_count):
        summed = image_blocks[column, c, line]
        for k in range(1, lines):
            along_copy(k, c).wait()
            summed = summed + image_last[k - 1, c]
        gradient_out[c] = summed / light_blocks[column, c, line]
    for copy in stores:
        copy.wait()


def local(
    stiffness, buoyancy_first, buoyancy_second, buoyancy_third, adjoint_before,
    adjoint_current, forward_field, traces, receiver_target, receiver_cell, source_cell,
):
    device_count = lax.axis_size(("shot", "sub"))
    sample_count = traces.shape[1]
    steps = forward_field.shape[1]
    depth, rows, length = stiffness.shape
    chunk_count = length // LANES
    row_count = traces.shape[0]
    capacity = max(2, (3 * row_count + 2 * device_count - 1) // (2 * device_count))
    slots = device_count * capacity

    subs = lax.axis_size("sub")
    rightward = [(i, i + 1) for i in range(subs - 1)]
    leftward = [(i + 1, i) for i in range(subs - 1)]
    left_halo = lax.ppermute(
        jnp.concatenate([adjoint_current[0, depth - HALO:], buoyancy_first[depth - 4:]], axis=0),
        "sub", rightward)
    right_halo = lax.ppermute(
        jnp.concatenate([adjoint_current[0, :HALO], buoyancy_first[:3]], axis=0), "sub", leftward)

    kernel = trace_kernel(sample_count, steps)
    values = jnp.dot(
        traces, kernel, precision=lax.Precision.HIGHEST, preferred_element_type=jnp.float32)
    target = receiver_target[:, 0]
    onehot = target[:, None] == jnp.arange(device_count, dtype=jnp.int32)[None, :]
    row_ids = jnp.arange(row_count, dtype=jnp.int32)
    lower = (row_ids[:, None] >= row_ids[None, :]).astype(jnp.bfloat16)
    running = jnp.dot(lower, onehot.astype(jnp.bfloat16), preferred_element_type=jnp.float32)
    slot = (jnp.sum(jnp.where(onehot, running, 0.0), axis=1) - 1.0).astype(jnp.int32)
    chosen = (
        (target * capacity + slot)[None, :] == jnp.arange(slots, dtype=jnp.int32)[:, None]
    ).astype(jnp.float32)
    rows_out = jnp.concatenate([values, receiver_cell.astype(jnp.float32)[:, None]], axis=1)
    packed = jnp.dot(
        chosen, rows_out, precision=lax.Precision.HIGHEST, preferred_element_type=jnp.float32)
    words = capacity * (steps + 1)
    lines_out = -(-words // LANES)
    mine = jnp.pad(packed.reshape(device_count, words), ((0, 0), (0, lines_out * LANES - words)))
    dma = pltpu.SemaphoreType.DMA
    in_vmem = pl.BlockSpec(memory_space=pltpu.VMEM)
    got = pl.pallas_call(
        functools.partial(exchange_body, lax.axis_size("shot"), lax.axis_size("sub")),
        out_shape=jax.ShapeDtypeStruct((device_count, lines_out, LANES), jnp.float32),
        in_specs=[in_vmem],
        out_specs=in_vmem,
        scratch_shapes=[dma((device_count - 1,)), dma((device_count - 1,))],
        compiler_params=pltpu.CompilerParams(collective_id=1, has_side_effects=True),
    )(mine.reshape(device_count, lines_out, LANES))
    got = got.reshape(device_count, -1)[:, :words].reshape(slots, steps + 1)
    groups = -(-slots // LANES)
    got = jnp.pad(got, ((0, groups * LANES - slots), (0, 0)))
    places = (got[:, steps] + 0.5).astype(jnp.int32)
    spots = places // LANES
    spot_rows = (spots % chunk_count) * (depth * rows) + spots // chunk_count
    lane_at = places % LANES
    turns = (lane_at - jnp.arange(groups * LANES, dtype=jnp.int32)) % LANES
    tiles = got[:, :steps].T.reshape(steps, groups, LANES).transpose(1, 0, 2)

    dense = pl.pallas_call(
        scatter_body,
        out_shape=jax.ShapeDtypeStruct((chunk_count * depth * rows, steps, LANES), jnp.float32),
        in_specs=[pl.BlockSpec(memory_space=pltpu.SMEM)] * 3
        + [pl.BlockSpec(memory_space=pltpu.VMEM)],
        out_specs=pl.BlockSpec(memory_space=pltpu.VMEM),
        cost_estimate=pl.CostEstimate(
            flops=16 * slots * steps * LANES, bytes_accessed=2**25, transcendentals=0),
        compiler_params=pltpu.CompilerParams(vmem_limit_bytes=14 * 2**20),
    )(spot_rows, lane_at, turns, tiles).reshape(chunk_count, depth, rows * steps, LANES)

    f32 = jnp.float32
    grid_shape = jax.ShapeDtypeStruct((depth, rows, length), f32)
    anywhere = pl.BlockSpec(memory_space=pl.ANY)
    cells = (chunk_count, depth, rows, LANES)
    shots = lax.axis_size("shot")
    lines = 4 if shots % 4 == 0 else 1
    columns = shots // lines
    part = depth * (rows // shots)
    shares = (columns, chunk_count, lines, part, LANES)
    gradient, earlier, latest = pl.pallas_call(
        functools.partial(wave_body, (steps, depth, rows, chunk_count, lines, columns)),
        out_shape=[jax.ShapeDtypeStruct((chunk_count, part, LANES), f32)] + [grid_shape] * 2,
        in_specs=[anywhere] * 9 + [in_vmem, pl.BlockSpec(memory_space=pltpu.SMEM)],
        out_specs=[pl.BlockSpec(memory_space=pltpu.VMEM)] + [anywhere] * 2,
        scratch_shapes=[
            pltpu.VMEM((2, chunk_count, depth + 2 * HALO, rows + 2 * PAD, LANES), f32),
            pltpu.VMEM(cells, f32),
            pltpu.VMEM((chunk_count, depth + 7, rows, LANES), f32),
            pltpu.VMEM(cells, f32),
            pltpu.VMEM(cells, f32),
            pltpu.VMEM(cells, f32),
            pltpu.VMEM(cells, f32),
            pltpu.VMEM((steps, depth, rows, length), jnp.bfloat16),
            pltpu.VMEM((chunk_count, rows + 2 * PAD, LANES), f32),
            pltpu.VMEM(shares, f32),
            pltpu.VMEM((shots - 1, chunk_count, part, LANES), f32),
            pltpu.VMEM(shares, f32),
            pltpu.VMEM((max(1, columns - 1),) + shares[1:], f32),
            pltpu.VMEM((max(1, lines - 1), chunk_count, part, LANES), f32),
            dma((10 * chunk_count + 1,)),
            dma((2 * chunk_count,)),
            dma((2, chunk_count, 2)),
            dma((2, chunk_count, 2)),
            dma((shots - 1,)),
            dma((shots - 1,)),
            dma((max(1, columns - 1), chunk_count)),
            dma((max(1, columns - 1), chunk_count)),
            dma((max(1, lines - 1), chunk_count)),
            dma((max(1, lines - 1), chunk_count)),
        ],
        compiler_params=pltpu.CompilerParams(
            collective_id=0, has_side_effects=True, vmem_limit_bytes=26 * 2**20),
    )(
        stiffness, buoyancy_first, buoyancy_second, buoyancy_third, adjoint_before[0],
        adjoint_current[0], forward_field[0], left_halo, right_halo, dense, source_cell[0],
    )
    gradient = gradient.reshape(chunk_count, depth, rows // shots, LANES)
    gradient = gradient.transpose(1, 2, 0, 3).reshape(depth, -1)
    return (gradient, earlier[None], latest[None])


def solution(mesh):
    placed = (
        P("sub", None, None),
        P("sub", None, None),
        P("sub", None, None),
        P("sub", None, None),
        P("shot", "sub", None, None),
        P("shot", "sub", None, None),
        P("shot", None, "sub", None, None),
        P(("shot", "sub"), None),
        P(("shot", "sub"), None),
        P(("shot", "sub")),
        P("shot", None),
    )
    return jax.shard_map(
        local,
        mesh=mesh,
        in_specs=placed,
        out_specs=(P("sub", "shot"), P("shot", "sub", None, None), P("shot", "sub", None, None)),
        check_vma=False,
    )
```

```python
import functools

import jax
import jax.numpy as jnp
from jax import lax
from jax.experimental import pallas as pl
from jax.experimental.pallas import tpu as pltpu
from jax.sharding import PartitionSpec as P

MUTE = 6
COEFFS = (1225.0 / 1024.0, -245.0 / 3072.0, 49.0 / 5120.0, -5.0 / 7168.0)
RATIOS = tuple(c / COEFFS[0] for c in COEFFS)
SCALE = COEFFS[0] * COEFFS[0]
DAMP = 0.1
LANES = 128
HALO = 7
PAD = 8
MESH = pl.DeviceIdType.MESH


def trace_kernel(sample_count, step_count):
    sample_pos = jnp.arange(sample_count, dtype=jnp.float32)[:, None]
    centers = (jnp.arange(step_count, dtype=jnp.float32)[None, :] + 0.5) * (
        sample_count / step_count
    )
    return 0.25 * jnp.exp(-jnp.abs(sample_pos - centers) / (sample_count / 8.0))


def weighted(pairs):
    total = pairs[0][0] - pairs[0][1]
    for ratio, (ahead, behind) in zip(RATIOS[1:], pairs[1:]):
        total = total + ratio * (ahead - behind)
    return total


def exchange_body(shots, subs, mine_ref, got_ref, send_sem, recv_sem):
    count = shots * subs
    me = lax.axis_index("shot") * subs + lax.axis_index("sub")

    def place(k):
        to = lax.rem(me + k, count)
        return {"shot": lax.div(to, subs), "sub": lax.rem(to, subs)}, to

    barrier = pltpu.get_barrier_semaphore()

    def greet(k, carry):
        pl.semaphore_signal(barrier, inc=1, device_id=place(k)[0], device_id_type=MESH)
        return carry

    lax.fori_loop(1, count, greet, 0)
    got_ref[count - 1] = mine_ref[me]
    pl.semaphore_wait(barrier, count - 1)

    def copy(k):
        device, to = place(k)
        return pltpu.make_async_remote_copy(
            mine_ref.at[to], got_ref.at[k - 1], send_sem.at[k - 1], recv_sem.at[k - 1],
            device_id=device, device_id_type=MESH)

    def send(k, carry):
        copy(k).start()
        return carry

    def finish(k, carry):
        copy(k).wait()
        return carry

    lax.fori_loop(1, count, send, 0)
    lax.fori_loop(1, count, finish, 0)


def scatter_body(row_ref, at_ref, turn_ref, value_ref, dense_ref):
    dense_ref[...] = jnp.zeros_like(dense_ref)
    lane = lax.broadcasted_iota(jnp.int32, (8, LANES), 1)

    def block(group, carry):
        tile = value_ref[group]

        def four(quad, inner):
            spots, terms, found = [], [], []
            for k in range(4):
                number = group * LANES + quad * 4 + k
                spots.append(row_ref[number])
                moved = pltpu.roll(tile, turn_ref[number], 1)
                terms.append(jnp.where(lane == at_ref[number], moved, 0.0))
                found.append(dense_ref[spots[k]])
            for k in range(4):
                total = found[k] + terms[k]
                for before in range(k):
                    same = jnp.where(spots[before] == spots[k], 1.0, 0.0)
                    total = total + terms[before] * same
                dense_ref[spots[k]] = total
            return inner

        return lax.fori_loop(0, LANES // 4, four, carry, unroll=4)

    lax.fori_loop(0, value_ref.shape[0], block, 0)


def wave_body(
    dims,
    stiff_hbm, first_hbm, second_hbm, third_hbm, before_hbm, current_hbm, forward_hbm,
    inject, source_ref,
    gradient_out, earlier_out, latest_out,
    field, stiff, first, second, third, partial, image, forward, flux,
    turned, flux_turned, third_turned,
    light_blocks, light_got, image_blocks, image_got, image_last,
    load_sem, store_sem, edge_send, edge_recv, face_send, face_recv,
    light_send, light_recv, across_send, across_recv, along_send, along_recv,
):
    steps, depth, rows, chunk_count, lines, columns = dims
    shots = lines * columns
    share = rows // shots
    shot = lax.axis_index("shot")
    line, column = lax.div(shot, columns), lax.rem(shot, columns)
    sub = lax.axis_index("sub")
    ends = lax.axis_size("sub") - 1
    has_left = sub > 0
    has_right = sub < ends
    zero_tile = jnp.zeros((8, LANES), jnp.float32)

    for c in range(chunk_count):
        def clear(plane, carry, c=c):
            for b in range(2):
                field[b, c, plane, 0:PAD, :] = zero_tile
                field[b, c, plane, PAD + rows:2 * PAD + rows, :] = zero_tile
            return carry
        lax.fori_loop(HALO, HALO + depth, clear, 0)
        for plane in list(range(HALO)) + list(range(HALO + depth, 2 * HALO + depth)):
            for b in range(2):
                field[b, c, plane] = jnp.zeros((2 * PAD + rows, LANES), jnp.float32)
        for face in list(range(4)) + list(range(4 + depth, 7 + depth)):
            first[c, face] = jnp.zeros((rows, LANES), jnp.float32)
        flux[c] = jnp.zeros((2 * PAD + rows, LANES), jnp.float32)

    barrier = pltpu.get_barrier_semaphore()

    @pl.when(has_left)
    def _():
        pl.semaphore_signal(barrier, inc=1, device_id={"sub": sub - 1}, device_id_type=MESH)

    @pl.when(has_right)
    def _():
        pl.semaphore_signal(barrier, inc=1, device_id={"sub": sub + 1}, device_id_type=MESH)

    for k in range(1, shots):
        pl.semaphore_signal(
            barrier, inc=1, device_id={"shot": lax.rem(shot + k, shots)}, device_id_type=MESH)

    def lanes(c):
        return pl.ds(c * LANES, LANES)

    inner = pl.ds(PAD, rows)
    loads = []

    def load(src, dst):
        copy = pltpu.make_async_copy(src, dst, load_sem.at[len(loads)])
        copy.start()
        loads.append(copy)

    for c in range(chunk_count):
        load(current_hbm.at[:, :, lanes(c)], field.at[0, c, pl.ds(HALO, depth), inner, :])
        load(third_hbm.at[:, :, lanes(c)], third.at[c])
        load(second_hbm.at[:, :, lanes(c)], second.at[c])
    early = len(loads)
    load(forward_hbm, forward)
    for c in range(chunk_count):
        load(first_hbm.at[:, :, lanes(c)], first.at[c, pl.ds(4, depth)])
        load(stiff_hbm.at[:, :, lanes(c)], stiff.at[c])
        load(before_hbm.at[:, :, lanes(c)], field.at[1, c, pl.ds(HALO, depth), inner, :])
    pl.semaphore_wait(
        barrier, (shots - 1) + jnp.where(has_left, 1, 0) + jnp.where(has_right, 1, 0))

    def face_copy(side, c):
        if side == 0:
            src = first_hbm.at[pl.ds(0, 3), :, lanes(c)]
            dst = first.at[c, pl.ds(4 + depth, 3)]
            to = sub - 1
        else:
            src = first_hbm.at[pl.ds(depth - 4, 4), :, lanes(c)]
            dst = first.at[c, pl.ds(0, 4)]
            to = sub + 1
        return pltpu.make_async_remote_copy(
            src, dst, face_send.at[side, c], face_recv.at[side, c],
            device_id={"sub": to}, device_id_type=MESH)

    def edge_copy(side, c, b, from_hbm=False):
        start = 0 if side == 0 else depth - HALO
        if from_hbm:
            src = current_hbm.at[pl.ds(start, HALO), :, lanes(c)]
        else:
            src = field.at[b, c, pl.ds(HALO + start, HALO), inner, :]
        dst = field.at[b, c, pl.ds(HALO + depth if side == 0 else 0, HALO), inner, :]
        return pltpu.make_async_remote_copy(
            src, dst, edge_send.at[side, c, b], edge_recv.at[side, c, b],
            device_id={"sub": sub - 1 if side == 0 else sub + 1}, device_id_type=MESH)

    sends_on = (has_left, has_right)
    gets_on = (has_right, has_left)
    for c in range(chunk_count):
        for side in range(2):
            @pl.when(sends_on[side])
            def _(side=side, c=c):
                edge_copy(side, c, 0, True).start()
                face_copy(side, c).start()
    base = PAD + lax.div(sub, lax.axis_size("sub"))
    for copy in loads[:early]:
        copy.wait()

    planes = LANES // rows
    tall = chunk_count * LANES

    def turn(tile):
        return tile.reshape(LANES, LANES).T

    def turn_faces(g, carry):
        for c in range(chunk_count):
            third_turned[g, c * LANES:(c + 1) * LANES, :] = turn(
                third[c, pl.ds(g * planes, planes)])
        return carry

    def third_part(b, g, carry):
        for c in range(chunk_count):
            turned[PAD + c * LANES:PAD + (c + 1) * LANES, :] = turn(
                field[b, c, pl.ds(HALO + g * planes, planes), PAD:PAD + rows, :])

        def out(i, inside):
            def near(s):
                return turned[pl.ds(PAD + i * 8 + s, 8), :]
            flux_turned[pl.ds(pl.multiple_of(PAD + i * 8, 8), 8), :] = (
                third_turned[g, pl.ds(pl.multiple_of(i * 8, 8), 8), :]
                * weighted([(near(k), near(1 - k)) for k in range(1, 5)]))
            return inside

        lax.fori_loop(0, tall // 8, out, 0, unroll=8)

        def back(i, inside):
            def near(s):
                return flux_turned[pl.ds(PAD + i * 8 + s, 8), :]
            turned[pl.ds(pl.multiple_of(PAD + i * 8, 8), 8), :] = weighted(
                [(near(k - 1), near(-k)) for k in range(1, 5)])
            return inside

        lax.fori_loop(0, tall // 8, back, 0, unroll=8)
        for c in range(chunk_count):
            partial[c, pl.ds(g * planes, planes)] = (
                turned[PAD + c * LANES:PAD + (c + 1) * LANES, :].T.reshape(planes, rows, LANES))
        return carry

    def inner_part(b, x, carry):
        for c in range(chunk_count):
            for y in range(0, rows, 8):
                def near(s, c=c, y=y):
                    return field[b, c, HALO + x, pl.ds(base + (y + s), 8), :]
                flux[c, pl.ds(PAD + y, 8), :] = second[c, x, pl.ds(y, 8), :] * weighted(
                    [(near(k), near(1 - k)) for k in range(1, 5)])
        for c in range(chunk_count):
            for y in range(0, rows, 8):
                def near(s, c=c, y=y):
                    return flux[c, pl.ds(base + (y + s), 8), :]
                at = pl.ds(y, 8)
                partial[c, x, at, :] = partial[c, x, at, :] + weighted(
                    [(near(k - 1), near(-k)) for k in range(1, 5)])
        return carry

    def inner_all(b):
        lax.fori_loop(0, depth // planes, functools.partial(third_part, b), 0)
        lax.fori_loop(0, depth, functools.partial(inner_part, b), 0)

    for start in (0, PAD + tall):
        turned[start:start + PAD, :] = zero_tile
        flux_turned[start:start + PAD, :] = zero_tile
    lax.fori_loop(0, depth // planes, turn_faces, 0)
    inner_all(0)
    for copy in loads[early:]:
        copy.wait()

    def put_blocks(blocks, c, x, value):
        for d in range(shots):
            blocks[d % columns, c, d // columns, pl.ds(x * share, share), :] = (
                value[d * share:(d + 1) * share, :])

    def prepare(x, carry):
        for c in range(chunk_count):
            stiff[c, x] = stiff[c, x] * SCALE
            total = jnp.zeros((rows, LANES), jnp.float32)
            for t in range(steps):
                frame = forward[t, x, :, c * LANES:(c + 1) * LANES].astype(jnp.float32)
                total = total + frame * frame
            put_blocks(light_blocks, c, x, total)
            image[c, x] = jnp.zeros((rows, LANES), jnp.float32)
        return carry

    lax.fori_loop(0, depth, prepare, 0)

    def light_copy(k):
        to = lax.rem(shot + k, shots)
        return pltpu.make_async_remote_copy(
            light_blocks.at[lax.rem(to, columns), :, lax.div(to, columns)],
            light_got.at[k - 1], light_send.at[k - 1], light_recv.at[k - 1],
            device_id={"shot": to}, device_id_type=MESH)

    for k in range(1, shots):
        light_copy(k).start()

    def across_copy(k, c):
        to = lax.rem(column + k, columns)
        return pltpu.make_async_remote_copy(
            image_blocks.at[to, c], image_got.at[k - 1, c],
            across_send.at[k - 1, c], across_recv.at[k - 1, c],
            device_id={"shot": line * columns + to}, device_id_type=MESH)

    def along_copy(k, c):
        to = lax.rem(line + k, lines)
        return pltpu.make_async_remote_copy(
            image_blocks.at[column, c, to], image_last.at[k - 1, c],
            along_send.at[k - 1, c], along_recv.at[k - 1, c],
            device_id={"shot": to * columns + column}, device_id_type=MESH)

    source = [source_ref[i].astype(jnp.float32) for i in range(3)]
    second_at = lax.broadcasted_iota(jnp.int32, (rows, LANES), 0).astype(jnp.float32) - source[1]
    third_at = lax.broadcasted_iota(jnp.int32, (rows, LANES), 1).astype(jnp.float32) - source[2]

    def mute(c, x, carry):
        first_at = (sub * depth + x).astype(jnp.float32) - source[0]
        along = third_at + float(c * LANES)
        distance = first_at * first_at + second_at * second_at + along * along
        put_blocks(
            image_blocks, c, x, image[c, x] * (1.0 - jnp.exp(-distance / (2.0 * MUTE * MUTE))))
        return carry

    for c in range(chunk_count):
        for side in range(2):
            @pl.when(gets_on[side])
            def _(side=side, c=c):
                face_copy(side, c).wait_recv()

            @pl.when(sends_on[side])
            def _(side=side, c=c):
                face_copy(side, c).wait_send()

    def outer_part(c, t, b, half, carry):
        y = pl.multiple_of(half * 16, 16)
        at = pl.ds(y, 16)
        wide = pl.ds(pl.multiple_of(PAD + y, 8), 16)
        p = [field[b, c, i, wide, :] for i in range(8)]
        q = []
        for f in range(-4, depth + 3):
            q.append(first[c, f + 4, at, :] * weighted([(p[3 + k], p[4 - k]) for k in range(1, 5)]))
            x = f - 3
            if x >= 0:
                div = weighted([(q[3 + k], q[4 - k]) for k in range(1, 5)]) + partial[c, x, at, :]
                change = stiff[c, x, at, :] * div + inject[c, x, pl.ds(t + 8 * y, 16, stride=8), :]
                now = p[0]
                past = field[1 - b, c, HALO + x, wide, :]
                field[1 - b, c, HALO + x, wide, :] = (now + now) - past + change
                frame = forward[t, x, at, c * LANES:(c + 1) * LANES].astype(jnp.float32)
                image[c, x, at, :] = image[c, x, at, :] + frame * change
                q = q[1:]
            if f + 1 < depth + 3:
                p = p[1:] + [field[b, c, f + 5 + HALO, wide, :]]
        return carry

    def one_step(t, carry):
        b = lax.rem(t, 2)

        @pl.when(t > 0)
        def _():
            inner_all(b)

        for c in range(chunk_count):
            for side in range(2):
                @pl.when(gets_on[side])
                def _(side=side, c=c):
                    edge_copy(side, c, b).wait_recv()

                @pl.when(sends_on[side])
                def _(side=side, c=c):
                    edge_copy(side, c, b).wait_send()

            lax.fori_loop(0, rows // 16, functools.partial(outer_part, c, t, b), 0)
            for side in range(2):
                @pl.when(jnp.logical_and(sends_on[side], t < steps - 1))
                def _(side=side, c=c):
                    edge_copy(side, c, 1 - b).start()

            @pl.when(t == steps - 1)
            def _(c=c):
                lax.fori_loop(0, depth, functools.partial(mute, c), 0)
                for k in range(1, columns):
                    across_copy(k, c).start()
        return carry

    lax.fori_loop(0, steps, one_step, 0)

    stores = []

    def store(src, dst):
        copy = pltpu.make_async_copy(src, dst, store_sem.at[len(stores)])
        copy.start()
        stores.append(copy)

    for c in range(chunk_count):
        body = pl.ds(HALO, depth)
        store(field.at[(steps - 1) % 2, c, body, inner, :], earlier_out.at[:, :, lanes(c)])
        store(field.at[steps % 2, c, body, inner, :], latest_out.at[:, :, lanes(c)])

    for k in range(1, shots):
        light_copy(k).wait()
    for c in range(chunk_count):
        light = light_blocks[column, c, line]
        for k in range(1, shots):
            light = light + light_got[k - 1, c]
        light_blocks[column, c, line] = light / (steps * shots) + DAMP
    for c in range(chunk_count):
        for k in range(1, columns):
            across_copy(k, c).wait()
            image_blocks[column, c] = image_blocks[column, c] + image_got[k - 1, c]
        for k in range(1, lines):
            along_copy(k, c).start()
    for c in range(chunk_count):
        summed = image_blocks[column, c, line]
        for k in range(1, lines):
            along_copy(k, c).wait()
            summed = summed + image_last[k - 1, c]
        gradient_out[c] = summed / light_blocks[column, c, line]
    for copy in stores:
        copy.wait()


def local(
    stiffness, buoyancy_first, buoyancy_second, buoyancy_third, adjoint_before,
    adjoint_current, forward_field, traces, receiver_target, receiver_cell, source_cell,
):
    device_count = lax.axis_size(("shot", "sub"))
    sample_count = traces.shape[1]
    steps = forward_field.shape[1]
    depth, rows, length = stiffness.shape
    chunk_count = length // LANES
    row_count = traces.shape[0]
    capacity = max(2, (3 * row_count + 2 * device_count - 1) // (2 * device_count))
    slots = device_count * capacity

    kernel = trace_kernel(sample_count, steps)
    values = jnp.dot(
        traces, kernel, precision=lax.Precision.HIGHEST, preferred_element_type=jnp.float32)
    target = receiver_target[:, 0]
    onehot = target[:, None] == jnp.arange(device_count, dtype=jnp.int32)[None, :]
    row_ids = jnp.arange(row_count, dtype=jnp.int32)
    lower = (row_ids[:, None] >= row_ids[None, :]).astype(jnp.bfloat16)
    running = jnp.dot(lower, onehot.astype(jnp.bfloat16), preferred_element_type=jnp.float32)
    slot = (jnp.sum(jnp.where(onehot, running, 0.0), axis=1) - 1.0).astype(jnp.int32)
    chosen = (
        (target * capacity + slot)[None, :] == jnp.arange(slots, dtype=jnp.int32)[:, None]
    ).astype(jnp.float32)
    rows_out = jnp.concatenate([values, receiver_cell.astype(jnp.float32)[:, None]], axis=1)
    packed = jnp.dot(
        chosen, rows_out, precision=lax.Precision.HIGHEST, preferred_element_type=jnp.float32)
    words = capacity * (steps + 1)
    lines_out = -(-words // LANES)
    mine = jnp.pad(packed.reshape(device_count, words), ((0, 0), (0, lines_out * LANES - words)))
    dma = pltpu.SemaphoreType.DMA
    in_vmem = pl.BlockSpec(memory_space=pltpu.VMEM)
    got = pl.pallas_call(
        functools.partial(exchange_body, lax.axis_size("shot"), lax.axis_size("sub")),
        out_shape=jax.ShapeDtypeStruct((device_count, lines_out, LANES), jnp.float32),
        in_specs=[in_vmem],
        out_specs=in_vmem,
        scratch_shapes=[dma((device_count - 1,)), dma((device_count - 1,))],
        compiler_params=pltpu.CompilerParams(collective_id=1, has_side_effects=True),
    )(mine.reshape(device_count, lines_out, LANES))
    got = got.reshape(device_count, -1)[:, :words].reshape(slots, steps + 1)
    groups = -(-slots // LANES)
    got = jnp.pad(got, ((0, groups * LANES - slots), (0, 0)))
    places = (got[:, steps] + 0.5).astype(jnp.int32)
    spots = places // LANES
    spot_rows = (spots % chunk_count) * (depth * rows) + spots // chunk_count
    lane_at = places % LANES
    turns = (lane_at - jnp.arange(groups * LANES, dtype=jnp.int32)) % LANES
    tiles = got[:, :steps].T.reshape(steps, groups, LANES).transpose(1, 0, 2)

    dense = pl.pallas_call(
        scatter_body,
        out_shape=jax.ShapeDtypeStruct((chunk_count * depth * rows, steps, LANES), jnp.float32),
        in_specs=[pl.BlockSpec(memory_space=pltpu.SMEM)] * 3
        + [pl.BlockSpec(memory_space=pltpu.VMEM)],
        out_specs=pl.BlockSpec(memory_space=pltpu.VMEM),
        cost_estimate=pl.CostEstimate(
            flops=16 * slots * steps * LANES, bytes_accessed=2**25, transcendentals=0),
        compiler_params=pltpu.CompilerParams(vmem_limit_bytes=14 * 2**20),
    )(spot_rows, lane_at, turns, tiles).reshape(chunk_count, depth, rows * steps, LANES)

    f32 = jnp.float32
    grid_shape = jax.ShapeDtypeStruct((depth, rows, length), f32)
    anywhere = pl.BlockSpec(memory_space=pl.ANY)
    cells = (chunk_count, depth, rows, LANES)
    shots = lax.axis_size("shot")
    lines = 4 if shots % 4 == 0 else 1
    columns = shots // lines
    part = depth * (rows // shots)
    shares = (columns, chunk_count, lines, part, LANES)
    gradient, earlier, latest = pl.pallas_call(
        functools.partial(wave_body, (steps, depth, rows, chunk_count, lines, columns)),
        out_shape=[jax.ShapeDtypeStruct((chunk_count, part, LANES), f32)] + [grid_shape] * 2,
        in_specs=[anywhere] * 7 + [in_vmem, pl.BlockSpec(memory_space=pltpu.SMEM)],
        out_specs=[pl.BlockSpec(memory_space=pltpu.VMEM)] + [anywhere] * 2,
        scratch_shapes=[
            pltpu.VMEM((2, chunk_count, depth + 2 * HALO, rows + 2 * PAD, LANES), f32),
            pltpu.VMEM(cells, f32),
            pltpu.VMEM((chunk_count, depth + 7, rows, LANES), f32),
            pltpu.VMEM(cells, f32),
            pltpu.VMEM(cells, f32),
            pltpu.VMEM(cells, f32),
            pltpu.VMEM(cells, f32),
            pltpu.VMEM((steps, depth, rows, length), jnp.bfloat16),
            pltpu.VMEM((chunk_count, rows + 2 * PAD, LANES), f32),
            pltpu.VMEM((length + 2 * PAD, LANES), f32),
            pltpu.VMEM((length + 2 * PAD, LANES), f32),
            pltpu.VMEM((depth * rows // LANES, length, LANES), f32),
            pltpu.VMEM(shares, f32),
            pltpu.VMEM((shots - 1, chunk_count, part, LANES), f32),
            pltpu.VMEM(shares, f32),
            pltpu.VMEM((max(1, columns - 1),) + shares[1:], f32),
            pltpu.VMEM((max(1, lines - 1), chunk_count, part, LANES), f32),
            dma((6 * chunk_count + 1,)),
            dma((2 * chunk_count,)),
            dma((2, chunk_count, 2)),
            dma((2, chunk_count, 2)),
            dma((2, chunk_count)),
            dma((2, chunk_count)),
            dma((shots - 1,)),
            dma((shots - 1,)),
            dma((max(1, columns - 1), chunk_count)),
            dma((max(1, columns - 1), chunk_count)),
            dma((max(1, lines - 1), chunk_count)),
            dma((max(1, lines - 1), chunk_count)),
        ],
        compiler_params=pltpu.CompilerParams(
            collective_id=0, has_side_effects=True, vmem_limit_bytes=26 * 2**20),
    )(
        stiffness, buoyancy_first, buoyancy_second, buoyancy_third, adjoint_before[0],
        adjoint_current[0], forward_field[0], dense, source_cell[0],
    )
    gradient = gradient.reshape(chunk_count, depth, rows // shots, LANES)
    gradient = gradient.transpose(1, 2, 0, 3).reshape(depth, -1)
    return (gradient, earlier[None], latest[None])


def solution(mesh):
    placed = (
        P("sub", None, None),
        P("sub", None, None),
        P("sub", None, None),
        P("sub", None, None),
        P("shot", "sub", None, None),
        P("shot", "sub", None, None),
        P("shot", None, "sub", None, None),
        P(("shot", "sub"), None),
        P(("shot", "sub"), None),
        P(("shot", "sub")),
        P("shot", None),
    )
    return jax.shard_map(
        local,
        mesh=mesh,
        in_specs=placed,
        out_specs=(P("sub", "shot"), P("shot", "sub", None, None), P("shot", "sub", None, None)),
        check_vma=False,
    )
```

```python
import functools

import jax
import jax.numpy as jnp
from jax import lax
from jax.experimental import pallas as pl
from jax.experimental.pallas import tpu as pltpu
from jax.sharding import PartitionSpec as P

MUTE = 6
COEFFS = (1225.0 / 1024.0, -245.0 / 3072.0, 49.0 / 5120.0, -5.0 / 7168.0)
RATIOS = tuple(c / COEFFS[0] for c in COEFFS)
SCALE = COEFFS[0] * COEFFS[0]
DAMP = 0.1
LANES = 128
HALO = 7
PAD = 8
MESH = pl.DeviceIdType.MESH


def trace_kernel(sample_count, step_count):
    sample_pos = jnp.arange(sample_count, dtype=jnp.float32)[:, None]
    centers = (jnp.arange(step_count, dtype=jnp.float32)[None, :] + 0.5) * (
        sample_count / step_count
    )
    return 0.25 * jnp.exp(-jnp.abs(sample_pos - centers) / (sample_count / 8.0))


def weighted(pairs):
    total = pairs[0][0] - pairs[0][1]
    for ratio, (ahead, behind) in zip(RATIOS[1:], pairs[1:]):
        total = total + ratio * (ahead - behind)
    return total


def exchange_body(shots, subs, mine_ref, got_ref, send_sem, recv_sem):
    count = shots * subs
    me = lax.axis_index("shot") * subs + lax.axis_index("sub")

    def place(k):
        to = lax.rem(me + k, count)
        return {"shot": lax.div(to, subs), "sub": lax.rem(to, subs)}, to

    barrier = pltpu.get_barrier_semaphore()

    def greet(k, carry):
        pl.semaphore_signal(barrier, inc=1, device_id=place(k)[0], device_id_type=MESH)
        return carry

    lax.fori_loop(1, count, greet, 0)
    got_ref[count - 1] = mine_ref[me]
    pl.semaphore_wait(barrier, count - 1)

    def copy(k):
        device, to = place(k)
        return pltpu.make_async_remote_copy(
            mine_ref.at[to], got_ref.at[k - 1], send_sem.at[k - 1], recv_sem.at[k - 1],
            device_id=device, device_id_type=MESH)

    def send(k, carry):
        copy(k).start()
        return carry

    def finish(k, carry):
        copy(k).wait()
        return carry

    lax.fori_loop(1, count, send, 0)
    lax.fori_loop(1, count, finish, 0)


def scatter_body(row_ref, at_ref, turn_ref, value_ref, dense_ref):
    dense_ref[...] = jnp.zeros_like(dense_ref)
    lane = lax.broadcasted_iota(jnp.int32, (8, LANES), 1)

    def block(group, carry):
        tile = value_ref[group]

        def four(quad, inner):
            spots, terms, found = [], [], []
            for k in range(4):
                number = group * LANES + quad * 4 + k
                spots.append(row_ref[number])
                moved = pltpu.roll(tile, turn_ref[number], 1)
                terms.append(jnp.where(lane == at_ref[number], moved, 0.0))
                found.append(dense_ref[spots[k]])
            for k in range(4):
                total = found[k] + terms[k]
                for before in range(k):
                    same = jnp.where(spots[before] == spots[k], 1.0, 0.0)
                    total = total + terms[before] * same
                dense_ref[spots[k]] = total
            return inner

        return lax.fori_loop(0, LANES // 4, four, carry, unroll=4)

    lax.fori_loop(0, value_ref.shape[0], block, 0)


def wave_body(
    dims,
    stiff_hbm, first_hbm, second_hbm, third_hbm, before_hbm, current_hbm, forward_hbm,
    inject, source_ref,
    gradient_out, earlier_out, latest_out,
    field, stiff, first, second, third, partial, image, forward, flux,
    turned, flux_turned, third_turned,
    light_blocks, light_got, image_blocks, image_got, image_last,
    load_sem, store_sem, edge_send, edge_recv, face_send, face_recv,
    light_send, light_recv, across_send, across_recv, along_send, along_recv,
):
    steps, depth, rows, chunk_count, lines, columns = dims
    shots = lines * columns
    share = rows // shots
    shot = lax.axis_index("shot")
    line, column = lax.div(shot, columns), lax.rem(shot, columns)
    sub = lax.axis_index("sub")
    ends = lax.axis_size("sub") - 1
    has_left = sub > 0
    has_right = sub < ends
    zero_tile = jnp.zeros((8, LANES), jnp.float32)

    for c in range(chunk_count):
        def clear(plane, carry, c=c):
            for b in range(2):
                field[b, c, plane, 0:PAD, :] = zero_tile
                field[b, c, plane, PAD + rows:2 * PAD + rows, :] = zero_tile
            return carry
        lax.fori_loop(HALO, HALO + depth, clear, 0)
        for plane in list(range(HALO)) + list(range(HALO + depth, 2 * HALO + depth)):
            for b in range(2):
                field[b, c, plane] = jnp.zeros((2 * PAD + rows, LANES), jnp.float32)
        for face in list(range(4)) + list(range(4 + depth, 7 + depth)):
            first[c, face] = jnp.zeros((rows, LANES), jnp.float32)
        flux[c] = jnp.zeros((2 * PAD + rows, LANES), jnp.float32)

    barrier = pltpu.get_barrier_semaphore()

    @pl.when(has_left)
    def _():
        pl.semaphore_signal(barrier, inc=1, device_id={"sub": sub - 1}, device_id_type=MESH)

    @pl.when(has_right)
    def _():
        pl.semaphore_signal(barrier, inc=1, device_id={"sub": sub + 1}, device_id_type=MESH)

    for k in range(1, shots):
        pl.semaphore_signal(
            barrier, inc=1, device_id={"shot": lax.rem(shot + k, shots)}, device_id_type=MESH)

    def lanes(c):
        return pl.ds(c * LANES, LANES)

    inner = pl.ds(PAD, rows)
    loads = []

    def load(src, dst):
        copy = pltpu.make_async_copy(src, dst, load_sem.at[len(loads)])
        copy.start()
        loads.append(copy)

    for c in range(chunk_count):
        load(current_hbm.at[:, :, lanes(c)], field.at[0, c, pl.ds(HALO, depth), inner, :])
        load(third_hbm.at[:, :, lanes(c)], third.at[c])
        load(second_hbm.at[:, :, lanes(c)], second.at[c])
    early = len(loads)
    load(forward_hbm, forward)
    for c in range(chunk_count):
        load(first_hbm.at[:, :, lanes(c)], first.at[c, pl.ds(4, depth)])
        load(stiff_hbm.at[:, :, lanes(c)], stiff.at[c])
        load(before_hbm.at[:, :, lanes(c)], field.at[1, c, pl.ds(HALO, depth), inner, :])
    pl.semaphore_wait(
        barrier, (shots - 1) + jnp.where(has_left, 1, 0) + jnp.where(has_right, 1, 0))

    def face_copy(side, c):
        if side == 0:
            src = first_hbm.at[pl.ds(0, 3), :, lanes(c)]
            dst = first.at[c, pl.ds(4 + depth, 3)]
            to = sub - 1
        else:
            src = first_hbm.at[pl.ds(depth - 4, 4), :, lanes(c)]
            dst = first.at[c, pl.ds(0, 4)]
            to = sub + 1
        return pltpu.make_async_remote_copy(
            src, dst, face_send.at[side, c], face_recv.at[side, c],
            device_id={"sub": to}, device_id_type=MESH)

    def edge_copy(side, c, b, from_hbm=False):
        start = 0 if side == 0 else depth - HALO
        if from_hbm:
            src = current_hbm.at[pl.ds(start, HALO), :, lanes(c)]
        else:
            src = field.at[b, c, pl.ds(HALO + start, HALO), inner, :]
        dst = field.at[b, c, pl.ds(HALO + depth if side == 0 else 0, HALO), inner, :]
        return pltpu.make_async_remote_copy(
            src, dst, edge_send.at[side, c, b], edge_recv.at[side, c, b],
            device_id={"sub": sub - 1 if side == 0 else sub + 1}, device_id_type=MESH)

    sends_on = (has_left, has_right)
    gets_on = (has_right, has_left)
    for c in range(chunk_count):
        for side in range(2):
            @pl.when(sends_on[side])
            def _(side=side, c=c):
                edge_copy(side, c, 0, True).start()
                face_copy(side, c).start()
    base = PAD + lax.div(sub, lax.axis_size("sub"))
    for copy in loads[:early]:
        copy.wait()

    planes = LANES // rows
    tall = chunk_count * LANES

    def turn(tile):
        return tile.reshape(LANES, LANES).T

    def turn_faces(g, carry):
        for c in range(chunk_count):
            third_turned[g, c * LANES:(c + 1) * LANES, :] = turn(
                third[c, pl.ds(g * planes, planes)])
        return carry

    def third_part(b, g, carry):
        for c in range(chunk_count):
            turned[PAD + c * LANES:PAD + (c + 1) * LANES, :] = turn(
                field[b, c, pl.ds(HALO + g * planes, planes), PAD:PAD + rows, :])

        def out(i, inside):
            def near(s):
                return turned[pl.ds(PAD + i * 8 + s, 8), :]
            flux_turned[pl.ds(pl.multiple_of(PAD + i * 8, 8), 8), :] = (
                third_turned[g, pl.ds(pl.multiple_of(i * 8, 8), 8), :]
                * weighted([(near(k), near(1 - k)) for k in range(1, 5)]))
            return inside

        lax.fori_loop(0, tall // 8, out, 0, unroll=16)

        def back(i, inside):
            def near(s):
                return flux_turned[pl.ds(PAD + i * 8 + s, 8), :]
            turned[pl.ds(pl.multiple_of(PAD + i * 8, 8), 8), :] = weighted(
                [(near(k - 1), near(-k)) for k in range(1, 5)])
            return inside

        lax.fori_loop(0, tall // 8, back, 0, unroll=16)
        for c in range(chunk_count):
            partial[c, pl.ds(g * planes, planes)] = (
                turned[PAD + c * LANES:PAD + (c + 1) * LANES, :].T.reshape(planes, rows, LANES))
        return carry

    def inner_part(b, x, carry):
        for c in range(chunk_count):
            for y in range(0, rows, 8):
                def near(s, c=c, y=y):
                    return field[b, c, HALO + x, pl.ds(base + (y + s), 8), :]
                flux[c, pl.ds(PAD + y, 8), :] = second[c, x, pl.ds(y, 8), :] * weighted(
                    [(near(k), near(1 - k)) for k in range(1, 5)])
        for c in range(chunk_count):
            for y in range(0, rows, 8):
                def near(s, c=c, y=y):
                    return flux[c, pl.ds(base + (y + s), 8), :]
                at = pl.ds(y, 8)
                partial[c, x, at, :] = partial[c, x, at, :] + weighted(
                    [(near(k - 1), near(-k)) for k in range(1, 5)])
        return carry

    def inner_all(b):
        lax.fori_loop(0, depth // planes, functools.partial(third_part, b), 0)
        lax.fori_loop(0, depth, functools.partial(inner_part, b), 0, unroll=2)

    for start in (0, PAD + tall):
        turned[start:start + PAD, :] = zero_tile
        flux_turned[start:start + PAD, :] = zero_tile
    lax.fori_loop(0, depth // planes, turn_faces, 0)
    inner_all(0)
    for copy in loads[early:]:
        copy.wait()

    def put_blocks(blocks, c, x, value):
        for d in range(shots):
            blocks[d % columns, c, d // columns, pl.ds(x * share, share), :] = (
                value[d * share:(d + 1) * share, :])

    def prepare(x, carry):
        for c in range(chunk_count):
            stiff[c, x] = stiff[c, x] * SCALE
            total = jnp.zeros((rows, LANES), jnp.float32)
            for t in range(steps):
                frame = forward[t, x, :, c * LANES:(c + 1) * LANES].astype(jnp.float32)
                total = total + frame * frame
            put_blocks(light_blocks, c, x, total)
            image[c, x] = jnp.zeros((rows, LANES), jnp.float32)
        return carry

    lax.fori_loop(0, depth, prepare, 0)

    def light_copy(k):
        to = lax.rem(shot + k, shots)
        return pltpu.make_async_remote_copy(
            light_blocks.at[lax.rem(to, columns), :, lax.div(to, columns)],
            light_got.at[k - 1], light_send.at[k - 1], light_recv.at[k - 1],
            device_id={"shot": to}, device_id_type=MESH)

    for k in range(1, shots):
        light_copy(k).start()

    def across_copy(k, c):
        to = lax.rem(column + k, columns)
        return pltpu.make_async_remote_copy(
            image_blocks.at[to, c], image_got.at[k - 1, c],
            across_send.at[k - 1, c], across_recv.at[k - 1, c],
            device_id={"shot": line * columns + to}, device_id_type=MESH)

    def along_copy(k, c):
        to = lax.rem(line + k, lines)
        return pltpu.make_async_remote_copy(
            image_blocks.at[column, c, to], image_last.at[k - 1, c],
            along_send.at[k - 1, c], along_recv.at[k - 1, c],
            device_id={"shot": to * columns + column}, device_id_type=MESH)

    source = [source_ref[i].astype(jnp.float32) for i in range(3)]
    second_at = lax.broadcasted_iota(jnp.int32, (rows, LANES), 0).astype(jnp.float32) - source[1]
    third_at = lax.broadcasted_iota(jnp.int32, (rows, LANES), 1).astype(jnp.float32) - source[2]

    def mute(c, x, carry):
        first_at = (sub * depth + x).astype(jnp.float32) - source[0]
        along = third_at + float(c * LANES)
        distance = first_at * first_at + second_at * second_at + along * along
        put_blocks(
            image_blocks, c, x, image[c, x] * (1.0 - jnp.exp(-distance / (2.0 * MUTE * MUTE))))
        return carry

    for c in range(chunk_count):
        for side in range(2):
            @pl.when(gets_on[side])
            def _(side=side, c=c):
                face_copy(side, c).wait_recv()

            @pl.when(sends_on[side])
            def _(side=side, c=c):
                face_copy(side, c).wait_send()

    def outer_part(c, t, b, half, carry):
        y = pl.multiple_of(half * 16, 16)
        at = pl.ds(y, 16)
        wide = pl.ds(pl.multiple_of(PAD + y, 8), 16)
        p = [field[b, c, i, wide, :] for i in range(8)]
        q = []
        for f in range(-4, depth + 3):
            q.append(first[c, f + 4, at, :] * weighted([(p[3 + k], p[4 - k]) for k in range(1, 5)]))
            x = f - 3
            if x >= 0:
                div = weighted([(q[3 + k], q[4 - k]) for k in range(1, 5)]) + partial[c, x, at, :]
                change = stiff[c, x, at, :] * div + inject[c, x, pl.ds(t + 8 * y, 16, stride=8), :]
                now = p[0]
                past = field[1 - b, c, HALO + x, wide, :]
                field[1 - b, c, HALO + x, wide, :] = (now + now) - past + change
                frame = forward[t, x, at, c * LANES:(c + 1) * LANES].astype(jnp.float32)
                image[c, x, at, :] = image[c, x, at, :] + frame * change
                q = q[1:]
            if f + 1 < depth + 3:
                p = p[1:] + [field[b, c, f + 5 + HALO, wide, :]]
        return carry

    def one_step(t, carry):
        b = lax.rem(t, 2)

        @pl.when(t > 0)
        def _():
            inner_all(b)

        for c in range(chunk_count):
            for side in range(2):
                @pl.when(gets_on[side])
                def _(side=side, c=c):
                    edge_copy(side, c, b).wait_recv()

                @pl.when(sends_on[side])
                def _(side=side, c=c):
                    edge_copy(side, c, b).wait_send()

            lax.fori_loop(0, rows // 16, functools.partial(outer_part, c, t, b), 0)
            for side in range(2):
                @pl.when(jnp.logical_and(sends_on[side], t < steps - 1))
                def _(side=side, c=c):
                    edge_copy(side, c, 1 - b).start()

            @pl.when(t == steps - 1)
            def _(c=c):
                lax.fori_loop(0, depth, functools.partial(mute, c), 0)
                for k in range(1, columns):
                    across_copy(k, c).start()
        return carry

    lax.fori_loop(0, steps, one_step, 0)

    stores = []

    def store(src, dst):
        copy = pltpu.make_async_copy(src, dst, store_sem.at[len(stores)])
        copy.start()
        stores.append(copy)

    for c in range(chunk_count):
        body = pl.ds(HALO, depth)
        store(field.at[(steps - 1) % 2, c, body, inner, :], earlier_out.at[:, :, lanes(c)])
        store(field.at[steps % 2, c, body, inner, :], latest_out.at[:, :, lanes(c)])

    for k in range(1, shots):
        light_copy(k).wait()
    for c in range(chunk_count):
        light = light_blocks[column, c, line]
        for k in range(1, shots):
            light = light + light_got[k - 1, c]
        light_blocks[column, c, line] = light / (steps * shots) + DAMP
    for c in range(chunk_count):
        for k in range(1, columns):
            across_copy(k, c).wait()
            image_blocks[column, c] = image_blocks[column, c] + image_got[k - 1, c]
        for k in range(1, lines):
            along_copy(k, c).start()
    for c in range(chunk_count):
        summed = image_blocks[column, c, line]
        for k in range(1, lines):
            along_copy(k, c).wait()
            summed = summed + image_last[k - 1, c]
        gradient_out[c] = summed / light_blocks[column, c, line]
    for copy in stores:
        copy.wait()


def local(
    stiffness, buoyancy_first, buoyancy_second, buoyancy_third, adjoint_before,
    adjoint_current, forward_field, traces, receiver_target, receiver_cell, source_cell,
):
    device_count = lax.axis_size(("shot", "sub"))
    sample_count = traces.shape[1]
    steps = forward_field.shape[1]
    depth, rows, length = stiffness.shape
    chunk_count = length // LANES
    row_count = traces.shape[0]
    capacity = max(2, (3 * row_count + 2 * device_count - 1) // (2 * device_count))
    slots = device_count * capacity

    kernel = trace_kernel(sample_count, steps)
    values = jnp.dot(
        traces, kernel, precision=lax.Precision.HIGHEST, preferred_element_type=jnp.float32)
    target = receiver_target[:, 0]
    onehot = target[:, None] == jnp.arange(device_count, dtype=jnp.int32)[None, :]
    row_ids = jnp.arange(row_count, dtype=jnp.int32)
    lower = (row_ids[:, None] >= row_ids[None, :]).astype(jnp.bfloat16)
    running = jnp.dot(lower, onehot.astype(jnp.bfloat16), preferred_element_type=jnp.float32)
    slot = (jnp.sum(jnp.where(onehot, running, 0.0), axis=1) - 1.0).astype(jnp.int32)
    chosen = (
        (target * capacity + slot)[None, :] == jnp.arange(slots, dtype=jnp.int32)[:, None]
    ).astype(jnp.float32)
    rows_out = jnp.concatenate([values, receiver_cell.astype(jnp.float32)[:, None]], axis=1)
    packed = jnp.dot(
        chosen, rows_out, precision=lax.Precision.HIGHEST, preferred_element_type=jnp.float32)
    words = capacity * (steps + 1)
    lines_out = -(-words // LANES)
    mine = jnp.pad(packed.reshape(device_count, words), ((0, 0), (0, lines_out * LANES - words)))
    dma = pltpu.SemaphoreType.DMA
    in_vmem = pl.BlockSpec(memory_space=pltpu.VMEM)
    got = pl.pallas_call(
        functools.partial(exchange_body, lax.axis_size("shot"), lax.axis_size("sub")),
        out_shape=jax.ShapeDtypeStruct((device_count, lines_out, LANES), jnp.float32),
        in_specs=[in_vmem],
        out_specs=in_vmem,
        scratch_shapes=[dma((device_count - 1,)), dma((device_count - 1,))],
        compiler_params=pltpu.CompilerParams(collective_id=1, has_side_effects=True),
    )(mine.reshape(device_count, lines_out, LANES))
    got = got.reshape(device_count, -1)[:, :words].reshape(slots, steps + 1)
    groups = -(-slots // LANES)
    got = jnp.pad(got, ((0, groups * LANES - slots), (0, 0)))
    places = (got[:, steps] + 0.5).astype(jnp.int32)
    spots = places // LANES
    spot_rows = (spots % chunk_count) * (depth * rows) + spots // chunk_count
    lane_at = places % LANES
    turns = (lane_at - jnp.arange(groups * LANES, dtype=jnp.int32)) % LANES
    tiles = got[:, :steps].T.reshape(steps, groups, LANES).transpose(1, 0, 2)

    dense = pl.pallas_call(
        scatter_body,
        out_shape=jax.ShapeDtypeStruct((chunk_count * depth * rows, steps, LANES), jnp.float32),
        in_specs=[pl.BlockSpec(memory_space=pltpu.SMEM)] * 3
        + [pl.BlockSpec(memory_space=pltpu.VMEM)],
        out_specs=pl.BlockSpec(memory_space=pltpu.VMEM),
        cost_estimate=pl.CostEstimate(
            flops=16 * slots * steps * LANES, bytes_accessed=2**25, transcendentals=0),
        compiler_params=pltpu.CompilerParams(vmem_limit_bytes=14 * 2**20),
    )(spot_rows, lane_at, turns, tiles).reshape(chunk_count, depth, rows * steps, LANES)

    f32 = jnp.float32
    grid_shape = jax.ShapeDtypeStruct((depth, rows, length), f32)
    anywhere = pl.BlockSpec(memory_space=pl.ANY)
    cells = (chunk_count, depth, rows, LANES)
    shots = lax.axis_size("shot")
    lines = 4 if shots % 4 == 0 else 1
    columns = shots // lines
    part = depth * (rows // shots)
    shares = (columns, chunk_count, lines, part, LANES)
    gradient, earlier, latest = pl.pallas_call(
        functools.partial(wave_body, (steps, depth, rows, chunk_count, lines, columns)),
        out_shape=[jax.ShapeDtypeStruct((chunk_count, part, LANES), f32)] + [grid_shape] * 2,
        in_specs=[anywhere] * 7 + [in_vmem, pl.BlockSpec(memory_space=pltpu.SMEM)],
        out_specs=[pl.BlockSpec(memory_space=pltpu.VMEM)] + [anywhere] * 2,
        scratch_shapes=[
            pltpu.VMEM((2, chunk_count, depth + 2 * HALO, rows + 2 * PAD, LANES), f32),
            pltpu.VMEM(cells, f32),
            pltpu.VMEM((chunk_count, depth + 7, rows, LANES), f32),
            pltpu.VMEM(cells, f32),
            pltpu.VMEM(cells, f32),
            pltpu.VMEM(cells, f32),
            pltpu.VMEM(cells, f32),
            pltpu.VMEM((steps, depth, rows, length), jnp.bfloat16),
            pltpu.VMEM((chunk_count, rows + 2 * PAD, LANES), f32),
            pltpu.VMEM((length + 2 * PAD, LANES), f32),
            pltpu.VMEM((length + 2 * PAD, LANES), f32),
            pltpu.VMEM((depth * rows // LANES, length, LANES), f32),
            pltpu.VMEM(shares, f32),
            pltpu.VMEM((shots - 1, chunk_count, part, LANES), f32),
            pltpu.VMEM(shares, f32),
            pltpu.VMEM((max(1, columns - 1),) + shares[1:], f32),
            pltpu.VMEM((max(1, lines - 1), chunk_count, part, LANES), f32),
            dma((6 * chunk_count + 1,)),
            dma((2 * chunk_count,)),
            dma((2, chunk_count, 2)),
            dma((2, chunk_count, 2)),
            dma((2, chunk_count)),
            dma((2, chunk_count)),
            dma((shots - 1,)),
            dma((shots - 1,)),
            dma((max(1, columns - 1), chunk_count)),
            dma((max(1, columns - 1), chunk_count)),
            dma((max(1, lines - 1), chunk_count)),
            dma((max(1, lines - 1), chunk_count)),
        ],
        compiler_params=pltpu.CompilerParams(
            collective_id=0, has_side_effects=True, vmem_limit_bytes=26 * 2**20),
    )(
        stiffness, buoyancy_first, buoyancy_second, buoyancy_third, adjoint_before[0],
        adjoint_current[0], forward_field[0], dense, source_cell[0],
    )
    gradient = gradient.reshape(chunk_count, depth, rows // shots, LANES)
    gradient = gradient.transpose(1, 2, 0, 3).reshape(depth, -1)
    return (gradient, earlier[None], latest[None])


def solution(mesh):
    placed = (
        P("sub", None, None),
        P("sub", None, None),
        P("sub", None, None),
        P("sub", None, None),
        P("shot", "sub", None, None),
        P("shot", "sub", None, None),
        P("shot", None, "sub", None, None),
        P(("shot", "sub"), None),
        P(("shot", "sub"), None),
        P(("shot", "sub")),
        P("shot", None),
    )
    return jax.shard_map(
        local,
        mesh=mesh,
        in_specs=placed,
        out_specs=(P("sub", "shot"), P("shot", "sub", None, None), P("shot", "sub", None, None)),
        check_vma=False,
    )
```
